32 devices in a mesh: var: 16 (over z, x, core), samp: 2 (over y).
Axes of the slice: x: 2, y: 2, z: 4, core: 2. Of those that a mesh axis runs over, the one named last changes fastest.
Arguments:
- observed: bfloat16 [1024, 16384], P('samp', 'var'), may hold values from -40 to 40
- pattern: int32 [128, 3], P('var'), may hold values from 0 to 127, as said below
- omega_init: bfloat16 [128, 3, 128, 128], P('var'), may hold values from -4 to 4
Outputs:
- precision: float32 [128, 3, 128, 128], P(('var', 'samp'))
The draws below stay inside these ranges and needn't reach their ends.
Inputs may be any that keep to these rules, and one draw needn't show every extreme that they name: pattern[R, 0] = R. The other two blocks of row block R belong to two different var devices among the four whose index differs from the owner of R by 1 or 2 (counted modulo the number of var devices). On every var device each of those four devices supplies the second block of exactly two of its row blocks.
All inputs are finite; a program needn't handle non-finite values.
Results may differ from the reference program's by a relative error of at most 0.0044.
Values may be sent and summed in bfloat16 or wider, within the bound.
A program may use at most 64 MiB of HBM per device.

```python
import jax
import jax.numpy as jnp
from jax import lax

BLK = 128
K = 3
ITERS = 2
ROWB = 8
ROWBLOCKS = 128
VARS = 16384
SAMPLES = 1024
N_VAR = 16


def draw_observed(key, part):
    key = jax.random.fold_in(key, 11)
    keys = jax.random.split(key, 2)
    positions = jnp.arange(VARS, dtype=jnp.float32) / VARS
    trends = 1.0 + 0.35 * positions
    spread = jax.random.uniform(keys[0], (VARS,), jnp.float32)
    scales = 0.5 * jnp.exp(jnp.log(10.0) * spread) * trends
    normals = jnp.clip(jax.random.normal(keys[1], (SAMPLES, VARS), jnp.float32), -5.0, 5.0)
    values = normals * scales
    return values.astype(jnp.bfloat16)


def draw_pattern(key, part):
    key = jax.random.fold_in(key, 23)
    keys = jax.random.split(key, 3)
    orders = jax.vmap(lambda single: jax.random.permutation(single, ROWB))(jax.random.split(keys[0], N_VAR))
    leading = orders.astype(jnp.int32) % 4
    trailing = (leading + 1 + jax.random.randint(keys[1], (N_VAR, ROWB), 0, 3)) % 4
    lead_offset = leading - 2 + (leading >= 2).astype(jnp.int32)
    trail_offset = trailing - 2 + (trailing >= 2).astype(jnp.int32)
    owners = jnp.arange(N_VAR, dtype=jnp.int32)[:, None]
    within = jax.random.randint(keys[2], (N_VAR, ROWB, 2), 0, ROWB)
    first_col = (owners + lead_offset + N_VAR) % N_VAR * ROWB + within[:, :, 0]
    second_col = (owners + trail_offset + N_VAR) % N_VAR * ROWB + within[:, :, 1]
    own_col = jnp.arange(ROWBLOCKS, dtype=jnp.int32).reshape(N_VAR, ROWB)
    return jnp.stack((own_col, first_col, second_col), axis=-1).reshape(ROWBLOCKS, K).astype(jnp.int32)


def draw_omega_init(key, part):
    key = jax.random.fold_in(key, 37)
    keys = jax.random.split(key, 2)
    values = 0.5 * jnp.clip(jax.random.normal(keys[0], (ROWBLOCKS, K, BLK, BLK), jnp.float32), -5.0, 5.0)
    diagonal = 2.0 * jnp.exp(jnp.log(2.0) * jax.random.uniform(keys[1], (ROWBLOCKS, BLK), jnp.float32))
    slot_ids = jnp.arange(K)[:, None, None]
    row_ids = jnp.arange(BLK)[None, :, None]
    col_ids = jnp.arange(BLK)[None, None, :]
    diag_mask = (slot_ids == 0) & (row_ids == col_ids)
    values = jnp.where(diag_mask[None], diagonal[:, None, :, None], values)
    return values.astype(jnp.bfloat16)


def setup_inputs(seed: int = 0) -> dict:
    key_of = jax.random.split(jax.random.key(seed), 4)
    observed = draw_observed(jax.random.fold_in(key_of[3], 71), 0)
    pattern = draw_pattern(jax.random.fold_in(key_of[3], 71), 0)
    omega_init = draw_omega_init(jax.random.fold_in(key_of[3], 71), 0)
    return dict(observed=observed, pattern=pattern, omega_init=omega_init)


STEP_SCALE = 0.5
THRESHOLD = 0.25
EPSILON = 1e-06

def proximal(iterate, grad, mean_sq, diag_mask):
    step_size = STEP_SCALE / jnp.sqrt(mean_sq + EPSILON)
    stepped = iterate - step_size * grad
    shrunk = stepped - jnp.clip(stepped, -THRESHOLD, THRESHOLD)
    barrier = 0.5 * (stepped + jnp.sqrt(stepped * stepped + 4.0 * step_size))
    return jnp.where(diag_mask, barrier, shrunk)

def settle(values):
    return lax.optimization_barrier(values.astype(jnp.bfloat16)).astype(jnp.float32)

def reference(observed, pattern, omega_init):
    blocks = observed.reshape(SAMPLES, VARS // BLK, BLK)
    slot_ids = lax.broadcasted_iota(jnp.int32, (K, BLK, BLK), 0)
    row_ids = lax.broadcasted_iota(jnp.int32, (K, BLK, BLK), 1)
    col_ids = lax.broadcasted_iota(jnp.int32, (K, BLK, BLK), 2)
    diag_mask = (slot_ids == 0) & (row_ids == col_ids)
    iterate = omega_init.astype(jnp.float32)
    for iteration in range(ITERS):
        packed = settle(iterate)

        def device_rows(operands):
            omega_rows, pattern_rows = operands
            chosen = jnp.take(blocks, pattern_rows.reshape(-1).astype(jnp.int32), axis=1)
            chosen = chosen.reshape(SAMPLES, ROWB, K, BLK).astype(jnp.float32)
            weighted = settle(jnp.einsum('rkab,nrkb->rna', omega_rows, chosen))
            return jnp.einsum('rna,nrkb->rkab', weighted, chosen) / SAMPLES
        grad = lax.map(device_rows, (packed.reshape(N_VAR, ROWB, K, BLK, BLK), pattern.reshape(N_VAR, ROWB, K)))
        grad = grad.reshape(ROWBLOCKS, K, BLK, BLK)
        mean_sq = jnp.mean(grad * grad)
        iterate = proximal(iterate, grad, mean_sq, diag_mask)
    return iterate
```

```python
import functools

import jax
import jax.numpy as jnp
from jax import lax
from jax.experimental import pallas as pl
from jax.experimental.pallas import tpu as pltpu
from jax.sharding import PartitionSpec as P

ITERS = 2


STEP_SCALE = 0.5
THRESHOLD = 0.25
EPSILON = 1e-06
CHUNKS = 4


def kernel(
    var_count,
    samp_count,
    obs_ref,
    pattern_ref,
    omega_ref,
    out_ref,
    *scratch,
):
    strips = scratch[:CHUNKS]
    (
        chosen,
        staged,
        gram_hi,
        gram_lo,
        gram,
        iterate,
        grads,
        near,
        far,
        x_send,
        x_recv,
        own_send,
        own_recv,
        pick_send,
        pick_recv,
        near_send,
        near_recv,
        far_send,
        far_recv,
    ) = scratch[CHUNKS:]
    v = lax.axis_index("var")
    s = lax.axis_index("samp")
    row_blocks, slot_count, size, _ = omega_ref.shape
    share = row_blocks // samp_count
    depth = strips[0].shape[1]
    width = slot_count * size
    inverse = 1.0 / (obs_ref.shape[0] * samp_count)
    entries = row_blocks * slot_count * size * size * var_count
    core = lax.rem(v, 2)
    group = 4 * samp_count
    layers = var_count // 4
    place = lax.rem(v, 4) * samp_count + s
    layer = v // 4

    def device(var, samp):
        return {"var": var, "samp": samp}

    def near_peer(d):
        other = lax.rem(place + d, group)
        return device(layer * 4 + other // samp_count, lax.rem(other, samp_count))

    def far_peer(d):
        return device(lax.rem(layer + d, layers) * 4 + lax.rem(v, 4), s)

    above = lax.rem(v + 2, var_count)
    below = lax.rem(v + var_count - 2, var_count)
    mate = v + 1 - 2 * core
    outside = lax.rem(v + var_count - 2 + 4 * (lax.rem(v, 4) // 2), var_count)

    barrier = pltpu.get_barrier_semaphore()
    for d in range(1, group):
        pl.semaphore_signal(barrier, inc=1, device_id=near_peer(d), device_id_type=pl.DeviceIdType.MESH)
    for d in range(1, layers):
        pl.semaphore_signal(barrier, inc=1, device_id=far_peer(d), device_id_type=pl.DeviceIdType.MESH)
    pl.semaphore_signal(barrier, inc=1, device_id=device(outside, s), device_id_type=pl.DeviceIdType.MESH)

    own = 2 * row_blocks
    for c in range(CHUNKS):
        for b in range(row_blocks):
            strips[c][own + b] = obs_ref[c * depth : (c + 1) * depth, b * size : (b + 1) * size]
    pl.semaphore_wait(barrier, group - 1 + layers - 1 + 1)

    pending = []

    def remote(src, dst, send, recv, target):
        copy = pltpu.make_async_remote_copy(
            src_ref=src,
            dst_ref=dst,
            send_sem=send,
            recv_sem=recv,
            device_id=target,
            device_id_type=pl.DeviceIdType.MESH,
        )
        copy.start()
        pending.append(copy)
        return copy

    def strip(c, slot):
        return strips[c].at[pl.ds(slot * row_blocks, row_blocks)]

    arrivals = [None] * CHUNKS

    def send_strip(c):
        up = remote(strip(c, 2), strip(c, 0), x_send.at[c, 0], x_recv.at[c, 0], device(above, s))
        down = remote(strip(c, 2), strip(c, 4), x_send.at[c, 1], x_recv.at[c, 1], device(below, s))
        side = remote(strip(c, 2), strip(c, 1 + 2 * core), x_send.at[c, 2], x_recv.at[c, 2], device(mate, s))
        arrivals[c] = (up, down, side)

    own_copies = {}

    def send_own(c):
        for d in range(1, samp_count):
            peer = lax.rem(s + d, samp_count)
            own_copies[c, d] = remote(
                strips[c].at[pl.ds(own + peer * share, share)],
                chosen.at[d, c, 0],
                own_send.at[d, c],
                own_recv.at[d, c],
                device(v, peer),
            )

    def slot_of(row, k):
        column = pattern_ref[row, k]
        owner = column // row_blocks
        offset = lax.rem(owner - v + var_count + 2, var_count)
        return jnp.minimum(offset, 4) * row_blocks + lax.rem(column, row_blocks)

    def add_gram(d, c, first):
        def one(r, carry):
            x = jnp.concatenate([chosen[d, c, k, r] for k in range(slot_count)], axis=1)
            product = lax.dot_general(x, x, (((0,), (0,)), ((), ())), preferred_element_type=jnp.float32)
            if first:
                gram[r] = product
            else:
                gram[r] += product
            return carry

        lax.fori_loop(0, share, one, 0)

    picks = {}

    def wait_picked(c):
        for d in range(1, samp_count):
            own_copies[c, d].wait_recv()
            picks[c, d].wait_recv()
            add_gram(d, c, False)

    send_strip(0)
    send_strip(1)
    for c in range(CHUNKS):
        send_own(c)
    for c in range(CHUNKS):
        up, down, side = arrivals[c]
        first = 1 - core
        pltpu.make_async_remote_copy(
            src_ref=strip(c, 2),
            dst_ref=strip(c, 4 * first),
            send_sem=x_send.at[c, 3],
            recv_sem=x_recv.at[c, first],
            device_id=device(mate, s),
            device_id_type=pl.DeviceIdType.MESH,
        ).wait_recv()
        forward = remote(
            strip(c, 4 * first), strip(c, 3 - 2 * core), x_send.at[c, 3], x_recv.at[c, 3], device(mate, s)
        )
        pltpu.make_async_remote_copy(
            src_ref=strip(c, 2),
            dst_ref=strip(c, 4 * core),
            send_sem=x_send.at[c, 3],
            recv_sem=x_recv.at[c, core],
            device_id=device(mate, s),
            device_id_type=pl.DeviceIdType.MESH,
        ).wait_recv()
        if c + 2 < CHUNKS:
            send_strip(c + 2)
        side.wait_recv()
        forward.wait_recv()
        for d in range(1, samp_count):
            peer = lax.rem(s + d, samp_count)

            def stage(r, carry):
                for k in range(1, slot_count):
                    staged[d - 1, c, k - 1, r] = strips[c][slot_of(peer * share + r, k)]
                return carry

            lax.fori_loop(0, share, stage, 0)
            picks[c, d] = remote(
                staged.at[d - 1, c],
                chosen.at[d, c, pl.ds(1, slot_count - 1)],
                pick_send.at[d, c],
                pick_recv.at[d, c],
                device(v, peer),
            )

        def keep(r, carry):
            chosen[0, c, 0, r] = strips[c][own + s * share + r]
            for k in range(1, slot_count):
                chosen[0, c, k, r] = strips[c][slot_of(s * share + r, k)]
            return carry

        lax.fori_loop(0, share, keep, 0)
        add_gram(0, c, c == 0)
        if c > 0:
            wait_picked(c - 1)
    wait_picked(CHUNKS - 1)

    def split(r, carry):
        full = gram[r]
        high = full.astype(jnp.bfloat16)
        gram_hi[r] = high
        gram_lo[r] = (full - high.astype(jnp.float32)).astype(jnp.bfloat16)
        for k in range(slot_count):
            iterate[r, :, k * size : (k + 1) * size] = omega_ref[s * share + r, k].astype(jnp.float32)
        return carry

    lax.fori_loop(0, share, split, 0)

    rows = lax.broadcasted_iota(jnp.int32, (size, width), 0)
    columns = lax.broadcasted_iota(jnp.int32, (size, width), 1)
    diagonal = rows == columns

    for step in range(ITERS):

        def descend(r, total):
            packed = iterate[r].astype(jnp.bfloat16)
            grad = jnp.dot(packed, gram_hi[r], preferred_element_type=jnp.float32)
            grad += jnp.dot(packed, gram_lo[r], preferred_element_type=jnp.float32)
            grad *= inverse
            grads[r] = grad
            square = grad * grad
            folded = square[:, :size]
            for k in range(1, slot_count):
                folded += square[:, k * size : (k + 1) * size]
            return total + jnp.sum(folded.reshape(size // 8, 8, size), axis=0)

        near[step, 0] = lax.fori_loop(0, share, descend, jnp.zeros((8, size), jnp.float32))
        copies = [
            remote(near.at[step, 0], near.at[step, d], near_send.at[step, d], near_recv.at[step, d], near_peer(d))
            for d in range(1, group)
        ]
        for copy in copies:
            copy.wait_recv()
        total = near[step, 0]
        for d in range(1, group):
            total += near[step, d]
        far[step, 0] = total
        copies = [
            remote(far.at[step, 0], far.at[step, d], far_send.at[step, d], far_recv.at[step, d], far_peer(d))
            for d in range(1, layers)
        ]
        for copy in copies:
            copy.wait_recv()
        for d in range(1, layers):
            total += far[step, d]
        mean_sq = jnp.sum(jnp.sum(total, axis=0, keepdims=True), axis=1, keepdims=True) / entries
        step_size = STEP_SCALE / jnp.sqrt(mean_sq + EPSILON)

        def advance(r, carry):
            stepped = iterate[r] - step_size * grads[r]
            shrunk = stepped - jnp.clip(stepped, -THRESHOLD, THRESHOLD)
            lifted = 0.5 * (stepped + jnp.sqrt(stepped * stepped + 4.0 * step_size))
            value = jnp.where(diagonal, lifted, shrunk)
            if step + 1 < ITERS:
                iterate[r] = value
            else:
                for k in range(slot_count):
                    out_ref[r, k] = value[:, k * size : (k + 1) * size]
            return carry

        lax.fori_loop(0, share, advance, 0)

    for copy in pending:
        copy.wait_send()


def body(observed, pattern, omega_init):
    var_count = lax.axis_size("var")
    samp_count = lax.axis_size("samp")
    row_blocks, slot_count, size, _ = omega_init.shape
    share = row_blocks // samp_count
    depth = observed.shape[0] // CHUNKS
    width = slot_count * size
    group = 4 * samp_count
    layers = var_count // 4
    dma = pltpu.SemaphoreType.DMA
    scratch = [pltpu.VMEM((5 * row_blocks, depth, size), jnp.bfloat16) for _ in range(CHUNKS)]
    scratch += [
        pltpu.VMEM((samp_count, CHUNKS, slot_count, share, depth, size), jnp.bfloat16),
        pltpu.VMEM((samp_count - 1, CHUNKS, slot_count - 1, share, depth, size), jnp.bfloat16),
        pltpu.VMEM((share, width, width), jnp.bfloat16),
        pltpu.VMEM((share, width, width), jnp.bfloat16),
        pltpu.VMEM((share, width, width), jnp.float32),
        pltpu.VMEM((share, size, width), jnp.float32),
        pltpu.VMEM((share, size, width), jnp.float32),
        pltpu.VMEM((ITERS, group, 8, size), jnp.float32),
        pltpu.VMEM((ITERS, layers, 8, size), jnp.float32),
        dma((CHUNKS, 4)),
        dma((CHUNKS, 4)),
        dma((samp_count, CHUNKS)),
        dma((samp_count, CHUNKS)),
        dma((samp_count, CHUNKS)),
        dma((samp_count, CHUNKS)),
        dma((ITERS, group)),
        dma((ITERS, group)),
        dma((ITERS, layers)),
        dma((ITERS, layers)),
    ]
    vmem = pl.BlockSpec(memory_space=pltpu.VMEM)
    return pl.pallas_call(
        functools.partial(kernel, var_count, samp_count),
        out_shape=jax.ShapeDtypeStruct((share, slot_count, size, size), jnp.float32),
        in_specs=[vmem, pl.BlockSpec(memory_space=pltpu.SMEM), vmem],
        out_specs=vmem,
        scratch_shapes=scratch,
        compiler_params=pltpu.CompilerParams(
            collective_id=0, has_side_effects=True, vmem_limit_bytes=40 * 1024 * 1024
        ),
    )(observed, pattern, omega_init)


def solution(mesh):
    return jax.shard_map(
        body,
        mesh=mesh,
        in_specs=(P("samp", "var"), P("var", None), P("var", None, None, None)),
        out_specs=P(("var", "samp"), None, None, None),
        check_vma=False,
    )
```

```python
import functools

import jax
import jax.numpy as jnp
from jax import lax
from jax.experimental import pallas as pl
from jax.experimental.pallas import tpu as pltpu
from jax.sharding import PartitionSpec as P

ITERS = 2


STEP_SCALE = 0.5
THRESHOLD = 0.25
EPSILON = 1e-06
CHUNKS = 4


def kernel(
    var_count,
    samp_count,
    obs_ref,
    pattern_ref,
    omega_ref,
    out_ref,
    *scratch,
):
    strips = scratch[:CHUNKS]
    (
        mine,
        theirs,
        staged,
        picked,
        omega,
        table,
        routes,
        gram_hi,
        gram_lo,
        gram,
        iterate,
        grads,
        near,
        far,
        load_sem,
        table_send,
        table_recv,
        x_send,
        x_recv,
        z_send,
        z_recv,
        mate_send,
        mate_recv,
        own_send,
        own_recv,
        pick_send,
        pick_recv,
        near_send,
        near_recv,
        far_send,
        far_recv,
    ) = scratch[CHUNKS:]
    v = lax.axis_index("var")
    s = lax.axis_index("samp")
    row_blocks, slot_count, size, _ = omega_ref.shape
    share = row_blocks // samp_count
    depth = strips[0].shape[1]
    half = depth * CHUNKS
    width = slot_count * size
    inverse = 1.0 / (obs_ref.shape[0] * samp_count)
    entries = row_blocks * slot_count * size * size * var_count
    core = lax.rem(v, 2)
    x = lax.rem(v, 4) // 2
    group = 4 * samp_count
    layers = var_count // 4
    place = lax.rem(v, 4) * samp_count + s
    layer = v // 4

    def device(var, samp):
        return {"var": var, "samp": samp}

    def near_peer(d):
        other = lax.rem(place + d, group)
        return device(layer * 4 + other // samp_count, lax.rem(other, samp_count))

    def far_peer(d):
        return device(lax.rem(layer + d, layers) * 4 + lax.rem(v, 4), s)

    mate = v + 1 - 2 * core
    across = v + 2 - 4 * x

    barrier = pltpu.get_barrier_semaphore()
    for d in range(1, group):
        pl.semaphore_signal(barrier, inc=1, device_id=near_peer(d), device_id_type=pl.DeviceIdType.MESH)
    for d in range(1, layers):
        pl.semaphore_signal(barrier, inc=1, device_id=far_peer(d), device_id_type=pl.DeviceIdType.MESH)

    loads = [
        pltpu.make_async_copy(obs_ref.at[:, pl.ds(b * size, size)], mine.at[b], load_sem.at[b])
        for b in range(row_blocks)
    ]
    load_table = pltpu.make_async_copy(pattern_ref, table.at[0], load_sem.at[row_blocks])
    load_omega = pltpu.make_async_copy(
        omega_ref.at[pl.ds(s * share, share)], omega, load_sem.at[row_blocks + 1]
    )
    load_table.start()
    for copy in loads:
        copy.start()
    load_omega.start()

    pending = []

    def remote(src, dst, send, recv, target):
        copy = pltpu.make_async_remote_copy(
            src_ref=src,
            dst_ref=dst,
            send_sem=send,
            recv_sem=recv,
            device_id=target,
            device_id_type=pl.DeviceIdType.MESH,
        )
        copy.start()
        pending.append(copy)
        return copy

    def strip(c, slot):
        return strips[c].at[pl.ds(slot * row_blocks, row_blocks)]

    def samples(side, c):
        return pl.ds(pl.multiple_of(side * half + c * depth, depth), depth)

    own_slot = 2 + 2 * x + core
    across_slot = 4 - 2 * x + core

    for copy in loads:
        copy.wait()
    pl.semaphore_wait(barrier, group - 1 + layers - 1)
    x_copies = [
        remote(mine.at[:, samples(1 - x, c)], strip(c, own_slot), x_send.at[c], x_recv.at[c], device(across, s))
        for c in range(CHUNKS)
    ]
    load_table.wait()
    table_copy = remote(table.at[0], table.at[1], table_send.at[0], table_recv.at[0], device(across, s))
    z_copies = []
    mate_copies = []
    for c in range(CHUNKS):
        strips[c][pl.ds(own_slot * row_blocks, row_blocks)] = mine[:, samples(x, c)]
        target = lax.rem(layer + layers - 1 + 2 * x, layers) * 4 + lax.rem(v, 4)
        z_copies.append(
            [
                remote(
                    strip(c, own_slot), strip(c, 6 - 6 * x + core), z_send.at[c, 0], z_recv.at[c, 0], device(target, s)
                )
            ]
        )
        mate_copies.append(
            [remote(strip(c, own_slot), strip(c, own_slot), mate_send.at[c, 0], mate_recv.at[c, 0], device(mate, s))]
        )
    own_copies = []
    for d in range(1, samp_count):
        peer = lax.rem(s + d, samp_count)
        own_copies.append(
            remote(mine.at[pl.ds(peer * share, share)], theirs.at[d], own_send.at[d], own_recv.at[d], device(v, peer))
        )

    def to_mate(c, kind, slot):
        mate_copies[c].append(
            remote(strip(c, slot), strip(c, slot), mate_send.at[c, kind], mate_recv.at[c, kind], device(mate, s))
        )

    def pass_on(c):
        x_copies[c].wait_recv()
        target = lax.rem(layer + layers + 1 - 2 * x, layers) * 4 + lax.rem(v, 4)
        z_copies[c].append(
            remote(strip(c, across_slot), strip(c, 6 * x + core), z_send.at[c, 1], z_recv.at[c, 1], device(target, s))
        )
        to_mate(c, 1, across_slot)

    def share_layers(c):
        for copy in z_copies[c]:
            copy.wait_recv()
        to_mate(c, 2, core)
        to_mate(c, 3, 6 + core)

    def block_of(e, row, k):
        column = routes[e, row, k]
        offset = lax.rem(column // row_blocks - layer * 4 + var_count + 2, var_count)
        return jnp.minimum(offset, 7) * row_blocks + lax.rem(column, row_blocks)

    picks = []

    def pick(c):
        for copy in mate_copies[c]:
            copy.wait_recv()
        sent = []
        for e, d in [(1, d) for d in range(samp_count)] + [(0, d) for d in range(samp_count)]:
            peer = lax.rem(s + d, samp_count)

            def stage(r, carry):
                for k in range(1, slot_count):
                    block = strips[c][block_of(e, peer * share + r, k)]
                    if e == 0 and d == 0:
                        picked[0, 0, c, k - 1, r] = block
                    else:
                        staged[e, d, c, k - 1, r] = block
                return carry

            lax.fori_loop(0, share, stage, 0)
            if e or d:
                sent.append(
                    remote(
                        staged.at[e, d, c],
                        picked.at[e, d, c],
                        pick_send.at[e, d, c],
                        pick_recv.at[e, d, c],
                        device(across if e else v, peer),
                    )
                )
        picks.append(sent)

    def add_gram(c):
        if c == 0:
            for copy in own_copies:
                copy.wait_recv()
        for copy in picks[c]:
            copy.wait_recv()

        def one(r, carry):
            parts = []
            for e in range(2):
                rows = samples(1 - x if e else x, c)
                for d in range(samp_count):
                    row_block = theirs[d, r, rows] if d else mine[s * share + r, rows]
                    parts.append(
                        jnp.concatenate([row_block] + [picked[e, d, c, k, r] for k in range(slot_count - 1)], axis=1)
                    )
            taken = jnp.concatenate(parts, axis=0)
            product = lax.dot_general(
                taken, taken, (((0,), (0,)), ((), ())), preferred_element_type=jnp.float32
            )
            if c == 0:
                gram[r] = product
            else:
                gram[r] += product
            return carry

        lax.fori_loop(0, share, one, 0)

    for turn in range(CHUNKS + 3):
        if turn < CHUNKS:
            pass_on(turn)
        if 0 <= turn - 1 < CHUNKS:
            share_layers(turn - 1)
        if turn == 1:
            table_copy.wait_recv()
            fetch = pltpu.make_async_copy(table, routes, load_sem.at[row_blocks + 2])
            fetch.start()
            fetch.wait()
        if 0 <= turn - 2 < CHUNKS:
            pick(turn - 2)
        if 0 <= turn - 3 < CHUNKS:
            add_gram(turn - 3)
    load_omega.wait()

    def split(r, carry):
        full = gram[r]
        high = full.astype(jnp.bfloat16)
        gram_hi[r] = high
        gram_lo[r] = (full - high.astype(jnp.float32)).astype(jnp.bfloat16)
        for k in range(slot_count):
            iterate[r, :, k * size : (k + 1) * size] = omega[r, k].astype(jnp.float32)
        return carry

    lax.fori_loop(0, share, split, 0)

    rows = lax.broadcasted_iota(jnp.int32, (size, width), 0)
    columns = lax.broadcasted_iota(jnp.int32, (size, width), 1)
    diagonal = rows == columns

    for step in range(ITERS):

        def descend(r, total):
            packed = iterate[r].astype(jnp.bfloat16)
            grad = jnp.dot(packed, gram_hi[r], preferred_element_type=jnp.float32)
            grad += jnp.dot(packed, gram_lo[r], preferred_element_type=jnp.float32)
            grad *= inverse
            grads[r] = grad
            square = grad * grad
            folded = square[:, :size]
            for k in range(1, slot_count):
                folded += square[:, k * size : (k + 1) * size]
            return total + jnp.sum(folded.reshape(size // 8, 8, size), axis=0)

        near[step, 0] = lax.fori_loop(0, share, descend, jnp.zeros((8, size), jnp.float32))
        copies = [
            remote(near.at[step, 0], near.at[step, d], near_send.at[step, d], near_recv.at[step, d], near_peer(d))
            for d in range(1, group)
        ]
        for copy in copies:
            copy.wait_recv()
        total = near[step, 0]
        for d in range(1, group):
            total += near[step, d]
        far[step, 0] = total
        copies = [
            remote(far.at[step, 0], far.at[step, d], far_send.at[step, d], far_recv.at[step, d], far_peer(d))
            for d in range(1, layers)
        ]
        for copy in copies:
            copy.wait_recv()
        for d in range(1, layers):
            total += far[step, d]
        mean_sq = jnp.sum(jnp.sum(total, axis=0, keepdims=True), axis=1, keepdims=True) / entries
        step_size = STEP_SCALE / jnp.sqrt(mean_sq + EPSILON)

        def advance(r, carry):
            stepped = iterate[r] - step_size * grads[r]
            shrunk = stepped - jnp.clip(stepped, -THRESHOLD, THRESHOLD)
            lifted = 0.5 * (stepped + jnp.sqrt(stepped * stepped + 4.0 * step_size))
            value = jnp.where(diagonal, lifted, shrunk)
            if step + 1 < ITERS:
                iterate[r] = value
            else:
                for k in range(slot_count):
                    out_ref[r, k] = value[:, k * size : (k + 1) * size]
            return carry

        lax.fori_loop(0, share, advance, 0)

    for copy in pending:
        copy.wait_send()


def body(observed, pattern, omega_init):
    var_count = lax.axis_size("var")
    samp_count = lax.axis_size("samp")
    row_blocks, slot_count, size, _ = omega_init.shape
    share = row_blocks // samp_count
    sample_rows = observed.shape[0]
    depth = sample_rows // (2 * CHUNKS)
    width = slot_count * size
    group = 4 * samp_count
    layers = var_count // 4
    dma = pltpu.SemaphoreType.DMA
    pattern = jnp.pad(pattern, ((0, 0), (0, size - slot_count)))
    scratch = [pltpu.VMEM((8 * row_blocks, depth, size), jnp.bfloat16) for _ in range(CHUNKS)]
    pick_shape = (2, samp_count, CHUNKS, slot_count - 1, share, depth, size)
    scratch += [
        pltpu.VMEM((row_blocks, sample_rows, size), jnp.bfloat16),
        pltpu.VMEM((samp_count, share, sample_rows, size), jnp.bfloat16),
        pltpu.VMEM(pick_shape, jnp.bfloat16),
        pltpu.VMEM(pick_shape, jnp.bfloat16),
        pltpu.VMEM((share, slot_count, size, size), jnp.bfloat16),
        pltpu.VMEM((2, row_blocks, size), jnp.int32),
        pltpu.SMEM((2, row_blocks, size), jnp.int32),
        pltpu.VMEM((share, width, width), jnp.bfloat16),
        pltpu.VMEM((share, width, width), jnp.bfloat16),
        pltpu.VMEM((share, width, width), jnp.float32),
        pltpu.VMEM((share, size, width), jnp.float32),
        pltpu.VMEM((share, size, width), jnp.float32),
        pltpu.VMEM((ITERS, group, 8, size), jnp.float32),
        pltpu.VMEM((ITERS, layers, 8, size), jnp.float32),
        dma((row_blocks + 3,)),
        dma((1,)),
        dma((1,)),
        dma((CHUNKS,)),
        dma((CHUNKS,)),
        dma((CHUNKS, 2)),
        dma((CHUNKS, 2)),
        dma((CHUNKS, 4)),
        dma((CHUNKS, 4)),
        dma((samp_count,)),
        dma((samp_count,)),
        dma((2, samp_count, CHUNKS)),
        dma((2, samp_count, CHUNKS)),
        dma((ITERS, group)),
        dma((ITERS, group)),
        dma((ITERS, layers)),
        dma((ITERS, layers)),
    ]
    hbm = pl.BlockSpec(memory_space=pl.ANY)
    return pl.pallas_call(
        functools.partial(kernel, var_count, samp_count),
        out_shape=jax.ShapeDtypeStruct((share, slot_count, size, size), jnp.float32),
        in_specs=[hbm, hbm, hbm],
        out_specs=pl.BlockSpec(memory_space=pltpu.VMEM),
        scratch_shapes=scratch,
        compiler_params=pltpu.CompilerParams(
            collective_id=0, has_side_effects=True, vmem_limit_bytes=56 * 1024 * 1024
        ),
    )(observed, pattern, omega_init)


def solution(mesh):
    return jax.shard_map(
        body,
        mesh=mesh,
        in_specs=(P("samp", "var"), P("var", None), P("var", None, None, None)),
        out_specs=P(("var", "samp"), None, None, None),
        check_vma=False,
    )
```

```python
import functools

import jax
import jax.numpy as jnp
from jax import lax
from jax.experimental import pallas as pl
from jax.experimental.pallas import tpu as pltpu
from jax.sharding import PartitionSpec as P

ITERS = 2


STEP_SCALE = 0.5
THRESHOLD = 0.25
EPSILON = 1e-06
CHUNKS = 4


def kernel(
    var_count,
    samp_count,
    obs_ref,
    pattern_ref,
    omega_ref,
    out_ref,
    *scratch,
):
    strips = scratch[:CHUNKS]
    (
        mine,
        theirs,
        staged,
        picked,
        omega,
        table,
        routes,
        gram_hi,
        gram_lo,
        gram,
        iterate,
        grads,
        near,
        far,
        load_sem,
        table_send,
        table_recv,
        x_send,
        x_recv,
        z_send,
        z_recv,
        mate_send,
        mate_recv,
        own_send,
        own_recv,
        pick_send,
        pick_recv,
        near_send,
        near_recv,
        far_send,
        far_recv,
    ) = scratch[CHUNKS:]
    v = lax.axis_index("var")
    s = lax.axis_index("samp")
    row_blocks, slot_count, size, _ = omega_ref.shape
    share = row_blocks // samp_count
    depth = strips[0].shape[1]
    half = depth * CHUNKS
    width = slot_count * size
    inverse = 1.0 / (obs_ref.shape[0] * samp_count)
    entries = row_blocks * slot_count * size * size * var_count
    core = lax.rem(v, 2)
    x = lax.rem(v, 4) // 2
    group = 4 * samp_count
    layers = var_count // 4
    place = lax.rem(v, 4) * samp_count + s
    layer = v // 4

    def device(var, samp):
        return {"var": var, "samp": samp}

    def near_peer(d):
        other = lax.rem(place + d, group)
        return device(layer * 4 + other // samp_count, lax.rem(other, samp_count))

    def far_peer(d):
        return device(lax.rem(layer + d, layers) * 4 + lax.rem(v, 4), s)

    mate = v + 1 - 2 * core
    across = v + 2 - 4 * x

    barrier = pltpu.get_barrier_semaphore()
    for d in range(1, group):
        pl.semaphore_signal(barrier, inc=1, device_id=near_peer(d), device_id_type=pl.DeviceIdType.MESH)
    for d in range(1, layers):
        pl.semaphore_signal(barrier, inc=1, device_id=far_peer(d), device_id_type=pl.DeviceIdType.MESH)

    loads = [
        pltpu.make_async_copy(obs_ref.at[:, pl.ds(b * size, size)], mine.at[b], load_sem.at[b])
        for b in range(row_blocks)
    ]
    load_table = pltpu.make_async_copy(pattern_ref, table.at[0], load_sem.at[row_blocks])
    load_omega = pltpu.make_async_copy(
        omega_ref.at[pl.ds(s * share, share)], omega, load_sem.at[row_blocks + 1]
    )
    load_table.start()
    for copy in loads:
        copy.start()
    load_omega.start()

    pending = []

    def remote(src, dst, send, recv, target):
        copy = pltpu.make_async_remote_copy(
            src_ref=src,
            dst_ref=dst,
            send_sem=send,
            recv_sem=recv,
            device_id=target,
            device_id_type=pl.DeviceIdType.MESH,
        )
        copy.start()
        pending.append(copy)
        return copy

    def strip(c, slot):
        return strips[c].at[pl.ds(slot * row_blocks, row_blocks)]

    def samples(side, c):
        return pl.ds(pl.multiple_of(side * half + c * depth, depth), depth)

    own_slot = 2 + 2 * x + core
    across_slot = 4 - 2 * x + core

    for copy in loads:
        copy.wait()
    pl.semaphore_wait(barrier, group - 1 + layers - 1)
    x_copies = []
    z_copies = []
    mate_copies = []

    def begin(c):
        x_copies.append(
            remote(mine.at[:, samples(1 - x, c)], strip(c, own_slot), x_send.at[c], x_recv.at[c], device(across, s))
        )
        strips[c][pl.ds(own_slot * row_blocks, row_blocks)] = mine[:, samples(x, c)]
        target = lax.rem(layer + layers - 1 + 2 * x, layers) * 4 + lax.rem(v, 4)
        z_copies.append(
            [
                remote(
                    strip(c, own_slot), strip(c, 6 - 6 * x + core), z_send.at[c, 0], z_recv.at[c, 0], device(target, s)
                )
            ]
        )
        mate_copies.append(
            [remote(strip(c, own_slot), strip(c, own_slot), mate_send.at[c, 0], mate_recv.at[c, 0], device(mate, s))]
        )

    begin(0)
    begin(1)
    load_table.wait()
    table_copy = remote(table.at[0], table.at[1], table_send.at[0], table_recv.at[0], device(across, s))
    own_copies = []
    for d in range(1, samp_count):
        peer = lax.rem(s + d, samp_count)
        own_copies.append(
            remote(mine.at[pl.ds(peer * share, share)], theirs.at[d], own_send.at[d], own_recv.at[d], device(v, peer))
        )

    def to_mate(c, kind, slot):
        mate_copies[c].append(
            remote(strip(c, slot), strip(c, slot), mate_send.at[c, kind], mate_recv.at[c, kind], device(mate, s))
        )

    def pass_on(c):
        x_copies[c].wait_recv()
        target = lax.rem(layer + layers + 1 - 2 * x, layers) * 4 + lax.rem(v, 4)
        z_copies[c].append(
            remote(strip(c, across_slot), strip(c, 6 * x + core), z_send.at[c, 1], z_recv.at[c, 1], device(target, s))
        )
        to_mate(c, 1, across_slot)
        if c + 2 < CHUNKS:
            begin(c + 2)

    def share_layers(c):
        for copy in z_copies[c]:
            copy.wait_recv()
        to_mate(c, 2, core)
        to_mate(c, 3, 6 + core)

    def block_of(e, row, k):
        column = routes[e, k, row]
        offset = lax.rem(column // row_blocks - layer * 4 + var_count + 2, var_count)
        return jnp.minimum(offset, 7) * row_blocks + lax.rem(column, row_blocks)

    picks = []

    def pick(c):
        for copy in mate_copies[c]:
            copy.wait_recv()
        sent = []
        for e, d in [(1, d) for d in range(samp_count)] + [(0, d) for d in range(samp_count)]:
            peer = lax.rem(s + d, samp_count)

            def stage(r, carry):
                for k in range(1, slot_count):
                    block = strips[c][block_of(e, peer * share + r, k)]
                    if e == 0 and d == 0:
                        picked[0, 0, c, k - 1, r] = block
                    else:
                        staged[e, d, c, k - 1, r] = block
                return carry

            lax.fori_loop(0, share, stage, 0)
            if e or d:
                sent.append(
                    remote(
                        staged.at[e, d, c],
                        picked.at[e, d, c],
                        pick_send.at[e, d, c],
                        pick_recv.at[e, d, c],
                        device(across if e else v, peer),
                    )
                )
        picks.append(sent)

    def add_gram(c):
        if c == 0:
            for copy in own_copies:
                copy.wait_recv()
        for copy in picks[c]:
            copy.wait_recv()

        def one(r, carry):
            parts = []
            for e in range(2):
                rows = samples(1 - x if e else x, c)
                for d in range(samp_count):
                    row_block = theirs[d, r, rows] if d else mine[s * share + r, rows]
                    parts.append(
                        jnp.concatenate([row_block] + [picked[e, d, c, k, r] for k in range(slot_count - 1)], axis=1)
                    )
            taken = jnp.concatenate(parts, axis=0)
            product = lax.dot_general(
                taken, taken, (((0,), (0,)), ((), ())), preferred_element_type=jnp.float32
            )
            if c == 0:
                gram[r] = product
            else:
                gram[r] += product
            return carry

        lax.fori_loop(0, share, one, 0)

    for turn in range(CHUNKS + 3):
        if turn < CHUNKS:
            pass_on(turn)
        if 0 <= turn - 1 < CHUNKS:
            share_layers(turn - 1)
        if turn == 1:
            table_copy.wait_recv()
            fetch = pltpu.make_async_copy(table, routes, load_sem.at[row_blocks + 2])
            fetch.start()
            fetch.wait()
        if 0 <= turn - 2 < CHUNKS:
            pick(turn - 2)
        if 0 <= turn - 3 < CHUNKS:
            add_gram(turn - 3)
    load_omega.wait()

    def split(r, carry):
        full = gram[r]
        high = full.astype(jnp.bfloat16)
        gram_hi[r] = high
        gram_lo[r] = (full - high.astype(jnp.float32)).astype(jnp.bfloat16)
        for k in range(slot_count):
            iterate[r, :, k * size : (k + 1) * size] = omega[r, k].astype(jnp.float32)
        return carry

    lax.fori_loop(0, share, split, 0)

    rows = lax.broadcasted_iota(jnp.int32, (size, width), 0)
    columns = lax.broadcasted_iota(jnp.int32, (size, width), 1)
    diagonal = rows == columns

    for step in range(ITERS):

        def descend(r, total):
            packed = iterate[r].astype(jnp.bfloat16)
            grad = jnp.dot(packed, gram_hi[r], preferred_element_type=jnp.float32)
            grad += jnp.dot(packed, gram_lo[r], preferred_element_type=jnp.float32)
            grad *= inverse
            grads[r] = grad
            square = grad * grad
            folded = square[:, :size]
            for k in range(1, slot_count):
                folded += square[:, k * size : (k + 1) * size]
            return total + jnp.sum(folded.reshape(size // 8, 8, size), axis=0)

        near[step, 0] = lax.fori_loop(0, share, descend, jnp.zeros((8, size), jnp.float32))
        copies = [
            remote(near.at[step, 0], near.at[step, d], near_send.at[step, d], near_recv.at[step, d], near_peer(d))
            for d in range(1, group)
        ]
        for copy in copies:
            copy.wait_recv()
        total = near[step, 0]
        for d in range(1, group):
            total += near[step, d]
        far[step, 0] = total
        copies = [
            remote(far.at[step, 0], far.at[step, d], far_send.at[step, d], far_recv.at[step, d], far_peer(d))
            for d in range(1, layers)
        ]
        for copy in copies:
            copy.wait_recv()
        for d in range(1, layers):
            total += far[step, d]
        mean_sq = jnp.sum(jnp.sum(total, axis=0, keepdims=True), axis=1, keepdims=True) / entries
        step_size = STEP_SCALE / jnp.sqrt(mean_sq + EPSILON)

        def advance(r, carry):
            stepped = iterate[r] - step_size * grads[r]
            shrunk = stepped - jnp.clip(stepped, -THRESHOLD, THRESHOLD)
            lifted = 0.5 * (stepped + jnp.sqrt(stepped * stepped + 4.0 * step_size))
            value = jnp.where(diagonal, lifted, shrunk)
            if step + 1 < ITERS:
                iterate[r] = value
            else:
                for k in range(slot_count):
                    out_ref[r, k] = value[:, k * size : (k + 1) * size]
            return carry

        lax.fori_loop(0, share, advance, 0)

    for copy in pending:
        copy.wait_send()


def body(observed, pattern, omega_init):
    var_count = lax.axis_size("var")
    samp_count = lax.axis_size("samp")
    row_blocks, slot_count, size, _ = omega_init.shape
    share = row_blocks // samp_count
    sample_rows = observed.shape[0]
    depth = sample_rows // (2 * CHUNKS)
    width = slot_count * size
    group = 4 * samp_count
    layers = var_count // 4
    dma = pltpu.SemaphoreType.DMA
    pattern = pattern.T
    scratch = [pltpu.VMEM((8 * row_blocks, depth, size), jnp.bfloat16) for _ in range(CHUNKS)]
    pick_shape = (2, samp_count, CHUNKS, slot_count - 1, share, depth, size)
    scratch += [
        pltpu.VMEM((row_blocks, sample_rows, size), jnp.bfloat16),
        pltpu.VMEM((samp_count, share, sample_rows, size), jnp.bfloat16),
        pltpu.VMEM(pick_shape, jnp.bfloat16),
        pltpu.VMEM(pick_shape, jnp.bfloat16),
        pltpu.VMEM((share, slot_count, size, size), jnp.bfloat16),
        pltpu.VMEM((2, slot_count, row_blocks), jnp.int32),
        pltpu.SMEM((2, slot_count, row_blocks), jnp.int32),
        pltpu.VMEM((share, width, width), jnp.bfloat16),
        pltpu.VMEM((share, width, width), jnp.bfloat16),
        pltpu.VMEM((share, width, width), jnp.float32),
        pltpu.VMEM((share, size, width), jnp.float32),
        pltpu.VMEM((share, size, width), jnp.float32),
        pltpu.VMEM((ITERS, group, 8, size), jnp.float32),
        pltpu.VMEM((ITERS, layers, 8, size), jnp.float32),
        dma((row_blocks + 3,)),
        dma((1,)),
        dma((1,)),
        dma((CHUNKS,)),
        dma((CHUNKS,)),
        dma((CHUNKS, 2)),
        dma((CHUNKS, 2)),
        dma((CHUNKS, 4)),
        dma((CHUNKS, 4)),
        dma((samp_count,)),
        dma((samp_count,)),
        dma((2, samp_count, CHUNKS)),
        dma((2, samp_count, CHUNKS)),
        dma((ITERS, group)),
        dma((ITERS, group)),
        dma((ITERS, layers)),
        dma((ITERS, layers)),
    ]
    hbm = pl.BlockSpec(memory_space=pltpu.HBM)
    return pl.pallas_call(
        functools.partial(kernel, var_count, samp_count),
        out_shape=jax.ShapeDtypeStruct((share, slot_count, size, size), jnp.float32),
        in_specs=[hbm, hbm, hbm],
        out_specs=pl.BlockSpec(memory_space=pltpu.VMEM),
        scratch_shapes=scratch,
        compiler_params=pltpu.CompilerParams(
            collective_id=0, has_side_effects=True, vmem_limit_bytes=53 * 1024 * 1024
        ),
    )(observed, pattern, omega_init)


def solution(mesh):
    return jax.shard_map(
        body,
        mesh=mesh,
        in_specs=(P("samp", "var"), P("var", None), P("var", None, None, None)),
        out_specs=P(("var", "samp"), None, None, None),
        check_vma=False,
    )
```

```python
import functools

import jax
import jax.numpy as jnp
from jax import lax
from jax.experimental import pallas as pl
from jax.experimental.pallas import tpu as pltpu
from jax.sharding import PartitionSpec as P

ITERS = 2


STEP_SCALE = 0.5
THRESHOLD = 0.25
EPSILON = 1e-06
CHUNKS = 8
AHEAD = 3


def kernel(
    var_count,
    samp_count,
    obs_ref,
    pattern_ref,
    omega_ref,
    out_ref,
    *scratch,
):
    strips = scratch[:CHUNKS]
    (
        mine,
        theirs,
        staged,
        picked,
        omega,
        table,
        routes,
        slots,
        gram_hi,
        gram_lo,
        gram,
        iterate,
        grads,
        near,
        far,
        load_sem,
        table_send,
        table_recv,
        x_send,
        x_recv,
        z_send,
        z_recv,
        mate_send,
        mate_recv,
        own_send,
        own_recv,
        pick_send,
        pick_recv,
        near_send,
        near_recv,
        far_send,
        far_recv,
    ) = scratch[CHUNKS:]
    v = lax.axis_index("var")
    s = lax.axis_index("samp")
    row_blocks, slot_count, size, _ = omega_ref.shape
    share = row_blocks // samp_count
    depth = strips[0].shape[1]
    half = depth * CHUNKS
    width = slot_count * size
    inverse = 1.0 / (obs_ref.shape[0] * samp_count)
    entries = row_blocks * slot_count * size * size * var_count
    core = lax.rem(v, 2)
    x = lax.rem(v, 4) // 2
    group = 4 * samp_count
    layers = var_count // 4
    place = lax.rem(v, 4) * samp_count + s
    layer = v // 4

    def device(var, samp):
        return {"var": var, "samp": samp}

    def near_peer(d):
        other = lax.rem(place + d, group)
        return device(layer * 4 + other // samp_count, lax.rem(other, samp_count))

    def far_peer(d):
        return device(lax.rem(layer + d, layers) * 4 + lax.rem(v, 4), s)

    mate = v + 1 - 2 * core
    across = v + 2 - 4 * x

    barrier = pltpu.get_barrier_semaphore()
    for d in range(1, group):
        pl.semaphore_signal(barrier, inc=1, device_id=near_peer(d), device_id_type=pl.DeviceIdType.MESH)
    for d in range(1, layers):
        pl.semaphore_signal(barrier, inc=1, device_id=far_peer(d), device_id_type=pl.DeviceIdType.MESH)

    loads = [
        pltpu.make_async_copy(obs_ref.at[:, pl.ds(b * size, size)], mine.at[b], load_sem.at[b])
        for b in range(row_blocks)
    ]
    load_table = pltpu.make_async_copy(pattern_ref, table.at[0], load_sem.at[row_blocks])
    load_omega = pltpu.make_async_copy(
        omega_ref.at[pl.ds(s * share, share)], omega, load_sem.at[row_blocks + 1]
    )
    load_table.start()
    for copy in loads:
        copy.start()
    load_omega.start()

    pending = []

    def remote(src, dst, send, recv, target):
        copy = pltpu.make_async_remote_copy(
            src_ref=src,
            dst_ref=dst,
            send_sem=send,
            recv_sem=recv,
            device_id=target,
            device_id_type=pl.DeviceIdType.MESH,
        )
        copy.start()
        pending.append(copy)
        return copy

    def strip(c, slot):
        return strips[c].at[pl.ds(slot * row_blocks, row_blocks)]

    def samples(side, c):
        return pl.ds(pl.multiple_of(side * half + c * depth, depth), depth)

    own_slot = 2 + 2 * x + core
    across_slot = 4 - 2 * x + core

    for copy in loads:
        copy.wait()
    pl.semaphore_wait(barrier, group - 1 + layers - 1)
    x_copies = []
    z_copies = []
    mate_copies = []

    def begin(c):
        x_copies.append(
            remote(mine.at[:, samples(1 - x, c)], strip(c, own_slot), x_send.at[c], x_recv.at[c], device(across, s))
        )
        strips[c][pl.ds(own_slot * row_blocks, row_blocks)] = mine[:, samples(x, c)]
        target = lax.rem(layer + layers - 1 + 2 * x, layers) * 4 + lax.rem(v, 4)
        z_copies.append(
            [
                remote(
                    strip(c, own_slot), strip(c, 6 - 6 * x + core), z_send.at[c, 0], z_recv.at[c, 0], device(target, s)
                )
            ]
        )
        mate_copies.append(
            [remote(strip(c, own_slot), strip(c, own_slot), mate_send.at[c, 0], mate_recv.at[c, 0], device(mate, s))]
        )

    for c in range(AHEAD):
        begin(c)
    load_table.wait()
    table_copy = remote(table.at[0], table.at[1], table_send.at[0], table_recv.at[0], device(across, s))
    own_copies = []
    for d in range(1, samp_count):
        peer = lax.rem(s + d, samp_count)
        own_copies.append(
            remote(mine.at[pl.ds(peer * share, share)], theirs.at[d], own_send.at[d], own_recv.at[d], device(v, peer))
        )

    def to_mate(c, kind, slot):
        mate_copies[c].append(
            remote(strip(c, slot), strip(c, slot), mate_send.at[c, kind], mate_recv.at[c, kind], device(mate, s))
        )

    def pass_on(c):
        x_copies[c].wait_recv()
        target = lax.rem(layer + layers + 1 - 2 * x, layers) * 4 + lax.rem(v, 4)
        z_copies[c].append(
            remote(strip(c, across_slot), strip(c, 6 * x + core), z_send.at[c, 1], z_recv.at[c, 1], device(target, s))
        )
        to_mate(c, 1, across_slot)
        if c + AHEAD < CHUNKS:
            begin(c + AHEAD)

    def share_layers(c):
        for copy in z_copies[c]:
            copy.wait_recv()
        to_mate(c, 2, core)
        to_mate(c, 3, 6 + core)

    def block_of(e, row, k):
        column = routes[e, k, row]
        offset = lax.rem(column // row_blocks - layer * 4 + var_count + 2, var_count)
        return jnp.minimum(offset, 7) * row_blocks + lax.rem(column, row_blocks)

    picks = []

    def pick(c):
        for copy in mate_copies[c]:
            copy.wait_recv()
        sent = []
        for e, d in [(1, d) for d in range(samp_count)] + [(0, d) for d in range(samp_count)]:
            peer = lax.rem(s + d, samp_count)
            for r in range(share):
                for k in range(1, slot_count):
                    block = strips[c][slots[e, d, k, r]]
                    if e == 0 and d == 0:
                        picked[0, 0, c, k - 1, r] = block
                    else:
                        staged[e, d, c, k - 1, r] = block
            if e or d:
                sent.append(
                    remote(
                        staged.at[e, d, c],
                        picked.at[e, d, c],
                        pick_send.at[e, d, c],
                        pick_recv.at[e, d, c],
                        device(across if e else v, peer),
                    )
                )
        picks.append(sent)

    def add_gram(c):
        if c == 0:
            for copy in own_copies:
                copy.wait_recv()
        for copy in picks[c]:
            copy.wait_recv()

        def one(r, carry):
            parts = []
            for e in range(2):
                rows = samples(1 - x if e else x, c)
                for d in range(samp_count):
                    row_block = theirs[d, r, rows] if d else mine[s * share + r, rows]
                    parts.append(
                        jnp.concatenate([row_block] + [picked[e, d, c, k, r] for k in range(slot_count - 1)], axis=1)
                    )
            taken = jnp.concatenate(parts, axis=0)
            product = lax.dot_general(
                taken, taken, (((0,), (0,)), ((), ())), preferred_element_type=jnp.float32
            )
            if c == 0:
                gram[r] = product
            else:
                gram[r] += product
            return carry

        lax.fori_loop(0, share, one, 0, unroll=True)

    for turn in range(CHUNKS + 4):
        if turn < CHUNKS:
            pass_on(turn)
        if 0 <= turn - 1 < CHUNKS:
            share_layers(turn - 1)
        if turn == 1:
            table_copy.wait_recv()
            fetch = pltpu.make_async_copy(table, routes, load_sem.at[row_blocks + 2])
            fetch.start()
            fetch.wait()
            for e in range(2):
                for d in range(samp_count):
                    for k in range(1, slot_count):
                        for r in range(share):
                            slots[e, d, k, r] = block_of(e, lax.rem(s + d, samp_count) * share + r, k)
        if 0 <= turn - 2 < CHUNKS:
            pick(turn - 2)
        if 0 <= turn - 4 < CHUNKS:
            add_gram(turn - 4)
    load_omega.wait()

    def split(r, carry):
        full = gram[r]
        high = full.astype(jnp.bfloat16)
        gram_hi[r] = high
        gram_lo[r] = (full - high.astype(jnp.float32)).astype(jnp.bfloat16)
        for k in range(slot_count):
            iterate[r, :, k * size : (k + 1) * size] = omega[r, k].astype(jnp.float32)
        return carry

    lax.fori_loop(0, share, split, 0, unroll=True)

    rows = lax.broadcasted_iota(jnp.int32, (size, size), 0)
    columns = lax.broadcasted_iota(jnp.int32, (size, size), 1)
    diagonal = rows == columns

    for step in range(ITERS):

        def descend(r, total):
            packed = iterate[r].astype(jnp.bfloat16)
            grad = jnp.dot(packed, gram_hi[r], preferred_element_type=jnp.float32)
            grad += jnp.dot(packed, gram_lo[r], preferred_element_type=jnp.float32)
            grad *= inverse
            grads[r] = grad
            square = grad * grad
            folded = square[:, :size]
            for k in range(1, slot_count):
                folded += square[:, k * size : (k + 1) * size]
            return total + jnp.sum(folded.reshape(size // 8, 8, size), axis=0)

        near[step, 0] = lax.fori_loop(
            0, share, descend, jnp.zeros((8, size), jnp.float32), unroll=True
        )
        copies = [
            remote(near.at[step, 0], near.at[step, d], near_send.at[step, d], near_recv.at[step, d], near_peer(d))
            for d in range(1, group)
        ]
        for copy in copies:
            copy.wait_recv()
        total = near[step, 0]
        for d in range(1, group):
            total += near[step, d]
        far[step, 0] = total
        copies = [
            remote(far.at[step, 0], far.at[step, d], far_send.at[step, d], far_recv.at[step, d], far_peer(d))
            for d in range(1, layers)
        ]
        for copy in copies:
            copy.wait_recv()
        for d in range(1, layers):
            total += far[step, d]
        mean_sq = jnp.sum(jnp.sum(total, axis=0, keepdims=True), axis=1, keepdims=True) / entries
        step_size = STEP_SCALE / jnp.sqrt(mean_sq + EPSILON)

        def advance(r, carry):
            for k in range(slot_count):
                lanes = slice(k * size, (k + 1) * size)
                stepped = iterate[r, :, lanes] - step_size * grads[r, :, lanes]
                value = stepped - jnp.clip(stepped, -THRESHOLD, THRESHOLD)
                if k == 0:
                    lifted = 0.5 * (stepped + jnp.sqrt(stepped * stepped + 4.0 * step_size))
                    value = jnp.where(diagonal, lifted, value)
                if step + 1 < ITERS:
                    iterate[r, :, lanes] = value
                else:
                    out_ref[r, k] = value
            return carry

        lax.fori_loop(0, share, advance, 0, unroll=True)

    for copy in pending:
        copy.wait_send()


def body(observed, pattern, omega_init):
    var_count = lax.axis_size("var")
    samp_count = lax.axis_size("samp")
    row_blocks, slot_count, size, _ = omega_init.shape
    share = row_blocks // samp_count
    sample_rows = observed.shape[0]
    depth = sample_rows // (2 * CHUNKS)
    width = slot_count * size
    group = 4 * samp_count
    layers = var_count // 4
    dma = pltpu.SemaphoreType.DMA
    pattern = pattern.T
    scratch = [pltpu.VMEM((8 * row_blocks, depth, size), jnp.bfloat16) for _ in range(CHUNKS)]
    pick_shape = (2, samp_count, CHUNKS, slot_count - 1, share, depth, size)
    scratch += [
        pltpu.VMEM((row_blocks, sample_rows, size), jnp.bfloat16),
        pltpu.VMEM((samp_count, share, sample_rows, size), jnp.bfloat16),
        pltpu.VMEM(pick_shape, jnp.bfloat16),
        pltpu.VMEM(pick_shape, jnp.bfloat16),
        pltpu.VMEM((share, slot_count, size, size), jnp.bfloat16),
        pltpu.VMEM((2, slot_count, row_blocks), jnp.int32),
        pltpu.SMEM((2, slot_count, row_blocks), jnp.int32),
        pltpu.SMEM((2, samp_count, slot_count, share), jnp.int32),
        pltpu.VMEM((share, width, width), jnp.bfloat16),
        pltpu.VMEM((share, width, width), jnp.bfloat16),
        pltpu.VMEM((share, width, width), jnp.float32),
        pltpu.VMEM((share, size, width), jnp.float32),
        pltpu.VMEM((share, size, width), jnp.float32),
        pltpu.VMEM((ITERS, group, 8, size), jnp.float32),
        pltpu.VMEM((ITERS, layers, 8, size), jnp.float32),
        dma((row_blocks + 3,)),
        dma((1,)),
        dma((1,)),
        dma((CHUNKS,)),
        dma((CHUNKS,)),
        dma((CHUNKS, 2)),
        dma((CHUNKS, 2)),
        dma((CHUNKS, 4)),
        dma((CHUNKS, 4)),
        dma((samp_count,)),
        dma((samp_count,)),
        dma((2, samp_count, CHUNKS)),
        dma((2, samp_count, CHUNKS)),
        dma((ITERS, group)),
        dma((ITERS, group)),
        dma((ITERS, layers)),
        dma((ITERS, layers)),
    ]
    hbm = pl.BlockSpec(memory_space=pltpu.HBM)
    return pl.pallas_call(
        functools.partial(kernel, var_count, samp_count),
        out_shape=jax.ShapeDtypeStruct((share, slot_count, size, size), jnp.float32),
        in_specs=[hbm, hbm, hbm],
        out_specs=pl.BlockSpec(memory_space=pltpu.VMEM),
        scratch_shapes=scratch,
        compiler_params=pltpu.CompilerParams(
            collective_id=0, has_side_effects=True, vmem_limit_bytes=53 * 1024 * 1024
        ),
    )(observed, pattern, omega_init)


def solution(mesh):
    return jax.shard_map(
        body,
        mesh=mesh,
        in_specs=(P("samp", "var"), P("var", None), P("var", None, None, None)),
        out_specs=P(("var", "samp"), None, None, None),
        check_vma=False,
    )
```

```python
import functools

import jax
import jax.numpy as jnp
from jax import lax
from jax.experimental import pallas as pl
from jax.experimental.pallas import tpu as pltpu
from jax.sharding import PartitionSpec as P

ITERS = 2


STEP_SCALE = 0.5
THRESHOLD = 0.25
EPSILON = 1e-06
CHUNKS = 8
AHEAD = 4


def kernel(
    var_count,
    samp_count,
    obs_ref,
    pattern_ref,
    omega_ref,
    out_ref,
    *scratch,
):
    strips = scratch[:CHUNKS]
    (
        mine,
        theirs,
        staged,
        picked,
        omega,
        table,
        routes,
        slots,
        gram_hi,
        gram_lo,
        gram,
        iterate,
        grads,
        near,
        far,
        load_sem,
        table_send,
        table_recv,
        x_send,
        x_recv,
        z_send,
        z_recv,
        mate_send,
        mate_recv,
        own_send,
        own_recv,
        pick_send,
        pick_recv,
        near_send,
        near_recv,
        far_send,
        far_recv,
    ) = scratch[CHUNKS:]
    v = lax.axis_index("var")
    s = lax.axis_index("samp")
    row_blocks, slot_count, size, _ = omega_ref.shape
    share = row_blocks // samp_count
    depth = strips[0].shape[1]
    half = depth * CHUNKS
    width = slot_count * size
    inverse = 1.0 / (obs_ref.shape[0] * samp_count)
    entries = row_blocks * slot_count * size * size * var_count
    core = lax.rem(v, 2)
    x = lax.rem(v, 4) // 2
    group = 4 * samp_count
    layers = var_count // 4
    place = lax.rem(v, 4) * samp_count + s
    layer = v // 4

    def device(var, samp):
        return {"var": var, "samp": samp}

    def near_peer(d):
        other = lax.rem(place + d, group)
        return device(layer * 4 + other // samp_count, lax.rem(other, samp_count))

    def far_peer(d):
        return device(lax.rem(layer + d, layers) * 4 + lax.rem(v, 4), s)

    mate = v + 1 - 2 * core
    across = v + 2 - 4 * x

    barrier = pltpu.get_barrier_semaphore()
    for d in range(1, group):
        pl.semaphore_signal(barrier, inc=1, device_id=near_peer(d), device_id_type=pl.DeviceIdType.MESH)
    for d in range(1, layers):
        pl.semaphore_signal(barrier, inc=1, device_id=far_peer(d), device_id_type=pl.DeviceIdType.MESH)

    loads = [
        pltpu.make_async_copy(obs_ref.at[:, pl.ds(b * size, size)], mine.at[b], load_sem.at[b])
        for b in range(row_blocks)
    ]
    load_table = pltpu.make_async_copy(pattern_ref, table.at[0], load_sem.at[row_blocks])
    load_omega = pltpu.make_async_copy(
        omega_ref.at[pl.ds(s * share, share)], omega, load_sem.at[row_blocks + 1]
    )
    load_table.start()
    for copy in loads:
        copy.start()
    load_omega.start()

    pending = []

    def remote(src, dst, send, recv, target):
        copy = pltpu.make_async_remote_copy(
            src_ref=src,
            dst_ref=dst,
            send_sem=send,
            recv_sem=recv,
            device_id=target,
            device_id_type=pl.DeviceIdType.MESH,
        )
        copy.start()
        pending.append(copy)
        return copy

    def strip(c, slot):
        return strips[c].at[pl.ds(slot * row_blocks, row_blocks)]

    def samples(side, c):
        return pl.ds(pl.multiple_of(side * half + c * depth, depth), depth)

    own_slot = 2 + 2 * x + core
    across_slot = 4 - 2 * x + core

    for copy in loads:
        copy.wait()
    pl.semaphore_wait(barrier, group - 1 + layers - 1)
    x_copies = []
    z_copies = []
    mate_copies = []

    def begin(c):
        x_copies.append(
            remote(mine.at[:, samples(1 - x, c)], strip(c, own_slot), x_send.at[c], x_recv.at[c], device(across, s))
        )
        strips[c][pl.ds(own_slot * row_blocks, row_blocks)] = mine[:, samples(x, c)]
        target = lax.rem(layer + layers - 1 + 2 * x, layers) * 4 + lax.rem(v, 4)
        z_copies.append(
            [
                remote(
                    strip(c, own_slot), strip(c, 6 - 6 * x + core), z_send.at[c, 0], z_recv.at[c, 0], device(target, s)
                )
            ]
        )
        mate_copies.append(
            [remote(strip(c, own_slot), strip(c, own_slot), mate_send.at[c, 0], mate_recv.at[c, 0], device(mate, s))]
        )

    for c in range(AHEAD):
        begin(c)
    load_table.wait()
    table_copy = remote(table.at[0], table.at[1], table_send.at[0], table_recv.at[0], device(across, s))
    own_copies = []
    for d in range(1, samp_count):
        peer = lax.rem(s + d, samp_count)
        own_copies.append(
            remote(mine.at[pl.ds(peer * share, share)], theirs.at[d], own_send.at[d], own_recv.at[d], device(v, peer))
        )

    def to_mate(c, kind, slot):
        mate_copies[c].append(
            remote(strip(c, slot), strip(c, slot), mate_send.at[c, kind], mate_recv.at[c, kind], device(mate, s))
        )

    def pass_on(c):
        x_copies[c].wait_recv()
        target = lax.rem(layer + layers + 1 - 2 * x, layers) * 4 + lax.rem(v, 4)
        z_copies[c].append(
            remote(strip(c, across_slot), strip(c, 6 * x + core), z_send.at[c, 1], z_recv.at[c, 1], device(target, s))
        )
        to_mate(c, 1, across_slot)
        if c + AHEAD < CHUNKS:
            begin(c + AHEAD)

    def share_layers(c):
        for copy in z_copies[c]:
            copy.wait_recv()
        to_mate(c, 2, core)
        to_mate(c, 3, 6 + core)

    def block_of(e, row, k):
        column = routes[e, k, row]
        offset = lax.rem(column // row_blocks - layer * 4 + var_count + 2, var_count)
        return jnp.minimum(offset, 7) * row_blocks + lax.rem(column, row_blocks)

    picks = []

    def pick(c):
        for copy in mate_copies[c]:
            copy.wait_recv()
        sent = []
        for e, d in [(1, d) for d in range(samp_count)] + [(0, d) for d in range(samp_count)]:
            peer = lax.rem(s + d, samp_count)
            for r in range(share):
                for k in range(1, slot_count):
                    block = strips[c][slots[e, d, k, r]]
                    if e == 0 and d == 0:
                        picked[0, 0, c, k - 1, r] = block
                    else:
                        staged[e, d, c, k - 1, r] = block
            if e or d:
                sent.append(
                    remote(
                        staged.at[e, d, c],
                        picked.at[e, d, c],
                        pick_send.at[e, d, c],
                        pick_recv.at[e, d, c],
                        device(across if e else v, peer),
                    )
                )
        picks.append(sent)

    def add_gram(c):
        if c == 0:
            for copy in own_copies:
                copy.wait_recv()
        for copy in picks[c]:
            copy.wait_recv()

        def one(r, carry):
            parts = []
            for e in range(2):
                rows = samples(1 - x if e else x, c)
                for d in range(samp_count):
                    row_block = theirs[d, r, rows] if d else mine[s * share + r, rows]
                    parts.append(
                        jnp.concatenate([row_block] + [picked[e, d, c, k, r] for k in range(slot_count - 1)], axis=1)
                    )
            taken = jnp.concatenate(parts, axis=0)
            product = lax.dot_general(
                taken, taken, (((0,), (0,)), ((), ())), preferred_element_type=jnp.float32
            )
            packed = jnp.concatenate([omega[r, k] for k in range(slot_count)], axis=1)
            weighted = lax.dot_general(
                packed, taken, (((1,), (1,)), ((), ())), preferred_element_type=jnp.float32
            ).astype(jnp.bfloat16)
            grad = jnp.dot(weighted, taken, preferred_element_type=jnp.float32)
            if c == 0:
                gram[r] = product
                grads[r] = grad
            else:
                gram[r] += product
                grads[r] += grad
            return carry

        lax.fori_loop(0, share, one, 0, unroll=True)

    for turn in range(CHUNKS + 5):
        if turn < CHUNKS:
            pass_on(turn)
        if turn == 1:
            table_copy.wait_recv()
            fetch = pltpu.make_async_copy(table, routes, load_sem.at[row_blocks + 2])
            fetch.start()
            fetch.wait()
            for e in range(2):
                for d in range(samp_count):
                    for k in range(1, slot_count):
                        for r in range(share):
                            slots[e, d, k, r] = block_of(e, lax.rem(s + d, samp_count) * share + r, k)
            load_omega.wait()
        if 0 <= turn - 2 < CHUNKS:
            share_layers(turn - 2)
        if 0 <= turn - 3 < CHUNKS:
            pick(turn - 3)
        if 0 <= turn - 5 < CHUNKS:
            add_gram(turn - 5)

    def split(r, carry):
        full = gram[r]
        high = full.astype(jnp.bfloat16)
        gram_hi[r] = high
        gram_lo[r] = (full - high.astype(jnp.float32)).astype(jnp.bfloat16)
        for k in range(slot_count):
            iterate[r, :, k * size : (k + 1) * size] = omega[r, k].astype(jnp.float32)
        return carry

    rows = lax.broadcasted_iota(jnp.int32, (size, size), 0)
    columns = lax.broadcasted_iota(jnp.int32, (size, size), 1)
    diagonal = rows == columns

    for step in range(ITERS):

        def descend(r, total):
            if step == 0:
                grad = grads[r]
            else:
                packed = iterate[r].astype(jnp.bfloat16)
                grad = jnp.dot(packed, gram_hi[r], preferred_element_type=jnp.float32)
                grad += jnp.dot(packed, gram_lo[r], preferred_element_type=jnp.float32)
            grad *= inverse
            grads[r] = grad
            square = grad * grad
            folded = square[:, :size]
            for k in range(1, slot_count):
                folded += square[:, k * size : (k + 1) * size]
            return total + jnp.sum(folded.reshape(size // 8, 8, size), axis=0)

        near[step, 0] = lax.fori_loop(
            0, share, descend, jnp.zeros((8, size), jnp.float32), unroll=True
        )
        copies = [
            remote(near.at[step, 0], near.at[step, d], near_send.at[step, d], near_recv.at[step, d], near_peer(d))
            for d in range(1, group)
        ]
        if step == 0:
            lax.fori_loop(0, share, split, 0, unroll=True)
        for copy in copies:
            copy.wait_recv()
        total = near[step, 0]
        for d in range(1, group):
            total += near[step, d]
        far[step, 0] = total
        copies = [
            remote(far.at[step, 0], far.at[step, d], far_send.at[step, d], far_recv.at[step, d], far_peer(d))
            for d in range(1, layers)
        ]
        for copy in copies:
            copy.wait_recv()
        for d in range(1, layers):
            total += far[step, d]
        mean_sq = jnp.sum(jnp.sum(total, axis=0, keepdims=True), axis=1, keepdims=True) / entries
        step_size = STEP_SCALE / jnp.sqrt(mean_sq + EPSILON)

        def advance(r, carry):
            for k in range(slot_count):
                lanes = slice(k * size, (k + 1) * size)
                stepped = iterate[r, :, lanes] - step_size * grads[r, :, lanes]
                value = stepped - jnp.clip(stepped, -THRESHOLD, THRESHOLD)
                if k == 0:
                    lifted = 0.5 * (stepped + jnp.sqrt(stepped * stepped + 4.0 * step_size))
                    value = jnp.where(diagonal, lifted, value)
                if step + 1 < ITERS:
                    iterate[r, :, lanes] = value
                else:
                    out_ref[r, k] = value
            return carry

        lax.fori_loop(0, share, advance, 0, unroll=True)

    for copy in pending:
        copy.wait_send()


def body(observed, pattern, omega_init):
    var_count = lax.axis_size("var")
    samp_count = lax.axis_size("samp")
    row_blocks, slot_count, size, _ = omega_init.shape
    share = row_blocks // samp_count
    sample_rows = observed.shape[0]
    depth = sample_rows // (2 * CHUNKS)
    width = slot_count * size
    group = 4 * samp_count
    layers = var_count // 4
    dma = pltpu.SemaphoreType.DMA
    pattern = pattern.T
    scratch = [pltpu.VMEM((8 * row_blocks, depth, size), jnp.bfloat16) for _ in range(CHUNKS)]
    pick_shape = (2, samp_count, CHUNKS, slot_count - 1, share, depth, size)
    scratch += [
        pltpu.VMEM((row_blocks, sample_rows, size), jnp.bfloat16),
        pltpu.VMEM((samp_count, share, sample_rows, size), jnp.bfloat16),
        pltpu.VMEM(pick_shape, jnp.bfloat16),
        pltpu.VMEM(pick_shape, jnp.bfloat16),
        pltpu.VMEM((share, slot_count, size, size), jnp.bfloat16),
        pltpu.VMEM((2, slot_count, row_blocks), jnp.int32),
        pltpu.SMEM((2, slot_count, row_blocks), jnp.int32),
        pltpu.SMEM((2, samp_count, slot_count, share), jnp.int32),
        pltpu.VMEM((share, width, width), jnp.bfloat16),
        pltpu.VMEM((share, width, width), jnp.bfloat16),
        pltpu.VMEM((share, width, width), jnp.float32),
        pltpu.VMEM((share, size, width), jnp.float32),
        pltpu.VMEM((share, size, width), jnp.float32),
        pltpu.VMEM((ITERS, group, 8, size), jnp.float32),
        pltpu.VMEM((ITERS, layers, 8, size), jnp.float32),
        dma((row_blocks + 3,)),
        dma((1,)),
        dma((1,)),
        dma((CHUNKS,)),
        dma((CHUNKS,)),
        dma((CHUNKS, 2)),
        dma((CHUNKS, 2)),
        dma((CHUNKS, 4)),
        dma((CHUNKS, 4)),
        dma((samp_count,)),
        dma((samp_count,)),
        dma((2, samp_count, CHUNKS)),
        dma((2, samp_count, CHUNKS)),
        dma((ITERS, group)),
        dma((ITERS, group)),
        dma((ITERS, layers)),
        dma((ITERS, layers)),
    ]
    hbm = pl.BlockSpec(memory_space=pltpu.HBM)
    return pl.pallas_call(
        functools.partial(kernel, var_count, samp_count),
        out_shape=jax.ShapeDtypeStruct((share, slot_count, size, size), jnp.float32),
        in_specs=[hbm, hbm, hbm],
        out_specs=pl.BlockSpec(memory_space=pltpu.VMEM),
        scratch_shapes=scratch,
        compiler_params=pltpu.CompilerParams(
            collective_id=0, has_side_effects=True, vmem_limit_bytes=53 * 1024 * 1024
        ),
    )(observed, pattern, omega_init)


def solution(mesh):
    return jax.shard_map(
        body,
        mesh=mesh,
        in_specs=(P("samp", "var"), P("var", None), P("var", None, None, None)),
        out_specs=P(("var", "samp"), None, None, None),
        check_vma=False,
    )
```

```python
import functools

import jax
import jax.numpy as jnp
from jax import lax
from jax.experimental import pallas as pl
from jax.experimental.pallas import tpu as pltpu
from jax.sharding import PartitionSpec as P

ITERS = 2


STEP_SCALE = 0.5
THRESHOLD = 0.25
EPSILON = 1e-06
CHUNKS = 8
AHEAD = 4


def kernel(
    var_count,
    samp_count,
    obs_ref,
    pattern_ref,
    omega_ref,
    out_ref,
    *scratch,
):
    strips = scratch[:CHUNKS]
    (
        mine,
        theirs,
        staged,
        picked,
        omega,
        table,
        routes,
        slots,
        gram_hi,
        gram_lo,
        gram,
        iterate,
        grads,
        near,
        far,
        load_sem,
        table_send,
        table_recv,
        x_send,
        x_recv,
        z_send,
        z_recv,
        mate_send,
        mate_recv,
        own_send,
        own_recv,
        pick_send,
        pick_recv,
        near_send,
        near_recv,
        far_send,
        far_recv,
    ) = scratch[CHUNKS:]
    v = lax.axis_index("var")
    s = lax.axis_index("samp")
    row_blocks, slot_count, size, _ = omega_ref.shape
    share = row_blocks // samp_count
    depth = strips[0].shape[1]
    half = depth * CHUNKS
    width = slot_count * size
    inverse = 1.0 / (obs_ref.shape[0] * samp_count)
    entries = row_blocks * slot_count * size * size * var_count
    core = lax.rem(v, 2)
    x = lax.rem(v, 4) // 2
    group = 4 * samp_count
    layers = var_count // 4
    place = lax.rem(v, 4) * samp_count + s
    layer = v // 4

    def device(var, samp):
        return {"var": var, "samp": samp}

    def near_peer(d):
        other = lax.rem(place + d, group)
        return device(layer * 4 + other // samp_count, lax.rem(other, samp_count))

    def far_peer(d):
        return device(lax.rem(layer + d, layers) * 4 + lax.rem(v, 4), s)

    mate = v + 1 - 2 * core
    across = v + 2 - 4 * x

    barrier = pltpu.get_barrier_semaphore()
    for d in range(1, group):
        pl.semaphore_signal(barrier, inc=1, device_id=near_peer(d), device_id_type=pl.DeviceIdType.MESH)
    for d in range(1, layers):
        pl.semaphore_signal(barrier, inc=1, device_id=far_peer(d), device_id_type=pl.DeviceIdType.MESH)

    loads = [
        pltpu.make_async_copy(obs_ref.at[:, pl.ds(b * size, size)], mine.at[b], load_sem.at[b])
        for b in range(row_blocks)
    ]
    load_table = pltpu.make_async_copy(pattern_ref, table.at[0], load_sem.at[row_blocks])
    load_omega = pltpu.make_async_copy(
        omega_ref.at[pl.ds(s * share, share)], omega, load_sem.at[row_blocks + 1]
    )
    load_table.start()
    for copy in loads:
        copy.start()
    load_omega.start()

    pending = []

    def remote(src, dst, send, recv, target):
        copy = pltpu.make_async_remote_copy(
            src_ref=src,
            dst_ref=dst,
            send_sem=send,
            recv_sem=recv,
            device_id=target,
            device_id_type=pl.DeviceIdType.MESH,
        )
        copy.start()
        pending.append(copy)
        return copy

    def strip(c, slot):
        return strips[c].at[pl.ds(slot * row_blocks, row_blocks)]

    def samples(side, c):
        return pl.ds(pl.multiple_of(side * half + c * depth, depth), depth)

    own_slot = core * 4 + 1 + x
    across_slot = core * 4 + 2 - x

    for copy in loads:
        copy.wait()
    pl.semaphore_wait(barrier, group - 1 + layers - 1)
    x_copies = []
    z_copies = []
    mate_copies = []

    def begin(c):
        x_copies.append(
            remote(mine.at[:, samples(1 - x, c)], strip(c, own_slot), x_send.at[c], x_recv.at[c], device(across, s))
        )
        strips[c][pl.ds(own_slot * row_blocks, row_blocks)] = mine[:, samples(x, c)]
        target = lax.rem(layer + layers - 1 + 2 * x, layers) * 4 + lax.rem(v, 4)
        z_copies.append(
            [
                remote(
                    strip(c, own_slot), strip(c, core * 4 + 3 - 3 * x), z_send.at[c, 0], z_recv.at[c, 0], device(target, s)
                )
            ]
        )

    for c in range(AHEAD):
        begin(c)
    load_table.wait()
    table_copy = remote(table.at[0], table.at[1], table_send.at[0], table_recv.at[0], device(across, s))
    own_copies = []
    for d in range(1, samp_count):
        peer = lax.rem(s + d, samp_count)
        own_copies.append(
            remote(mine.at[pl.ds(peer * share, share)], theirs.at[d], own_send.at[d], own_recv.at[d], device(v, peer))
        )

    def pass_on(c):
        x_copies[c].wait_recv()
        target = lax.rem(layer + layers + 1 - 2 * x, layers) * 4 + lax.rem(v, 4)
        z_copies[c].append(
            remote(strip(c, across_slot), strip(c, core * 4 + 3 * x), z_send.at[c, 1], z_recv.at[c, 1], device(target, s))
        )
        if c + AHEAD < CHUNKS:
            begin(c + AHEAD)

    def share_layers(c):
        for copy in z_copies[c]:
            copy.wait_recv()
        all_mine = strips[c].at[pl.ds(core * 4 * row_blocks, 4 * row_blocks)]
        mate_copies.append(remote(all_mine, all_mine, mate_send.at[c], mate_recv.at[c], device(mate, s)))

    def block_of(e, row, k):
        column = routes[e, k, row]
        offset = lax.rem(column // row_blocks - layer * 4 + var_count + 2, var_count)
        offset = jnp.minimum(offset, 7)
        return (lax.rem(offset, 2) * 4 + offset // 2) * row_blocks + lax.rem(column, row_blocks)

    picks = []

    def pick(c):
        mate_copies[c].wait_recv()
        sent = []
        for e, d in [(1 - e, samp_count - 1 - d) for e in range(2) for d in range(samp_count)]:
            peer = lax.rem(s + d, samp_count)
            for r in range(share):
                for k in range(1, slot_count):
                    block = strips[c][slots[e, d, k, r]]
                    if e == 0 and d == 0:
                        picked[0, 0, c, k - 1, r] = block
                    else:
                        staged[e, d, c, k - 1, r] = block
            if e or d:
                sent.append(
                    remote(
                        staged.at[e, d, c],
                        picked.at[e, d, c],
                        pick_send.at[e, d, c],
                        pick_recv.at[e, d, c],
                        device(across if e else v, peer),
                    )
                )
        picks.append(sent)

    def take(c, r):
        parts = []
        for e in range(2):
            rows = samples(1 - x if e else x, c)
            for d in range(samp_count):
                row_block = theirs[d, r, rows] if d else mine[s * share + r, rows]
                parts.append(
                    jnp.concatenate([row_block] + [picked[e, d, c, k, r] for k in range(slot_count - 1)], axis=1)
                )
        return jnp.concatenate(parts, axis=0)

    def add_grad(c):
        if c == 0:
            for copy in own_copies:
                copy.wait_recv()
        for copy in picks[c]:
            copy.wait_recv()
        for r in range(share):
            taken = take(c, r)
            packed = jnp.concatenate([omega[r, k] for k in range(slot_count)], axis=1)
            weighted = lax.dot_general(
                packed, taken, (((1,), (1,)), ((), ())), preferred_element_type=jnp.float32
            ).astype(jnp.bfloat16)
            grad = jnp.dot(weighted, taken, preferred_element_type=jnp.float32)
            if c == 0:
                grads[r] = grad
            else:
                grads[r] += grad

    def add_gram(c):
        for r in range(share):
            taken = take(c, r)
            product = lax.dot_general(
                taken, taken, (((0,), (0,)), ((), ())), preferred_element_type=jnp.float32
            )
            if c == 0:
                gram[r] = product
            else:
                gram[r] += product

    for turn in range(CHUNKS + 5):
        if turn < CHUNKS:
            pass_on(turn)
        if turn == 1:
            table_copy.wait_recv()
            fetch = pltpu.make_async_copy(table, routes, load_sem.at[row_blocks + 2])
            fetch.start()
            fetch.wait()
            for e in range(2):
                for d in range(samp_count):
                    for k in range(1, slot_count):
                        for r in range(share):
                            slots[e, d, k, r] = block_of(e, lax.rem(s + d, samp_count) * share + r, k)
            load_omega.wait()
        if 0 <= turn - 2 < CHUNKS:
            share_layers(turn - 2)
        if 0 <= turn - 3 < CHUNKS:
            pick(turn - 3)
        if 0 <= turn - 5 < CHUNKS:
            add_grad(turn - 5)
            if turn - 5 < CHUNKS - 1:
                add_gram(turn - 5)

    def split(r, carry):
        full = gram[r]
        high = full.astype(jnp.bfloat16)
        gram_hi[r] = high
        gram_lo[r] = (full - high.astype(jnp.float32)).astype(jnp.bfloat16)
        for k in range(slot_count):
            iterate[r, :, k * size : (k + 1) * size] = omega[r, k].astype(jnp.float32)
        return carry

    rows = lax.broadcasted_iota(jnp.int32, (size, size), 0)
    columns = lax.broadcasted_iota(jnp.int32, (size, size), 1)
    diagonal = rows == columns

    for step in range(ITERS):

        def descend(r, total):
            if step == 0:
                grad = grads[r]
            else:
                packed = iterate[r].astype(jnp.bfloat16)
                grad = jnp.dot(packed, gram_hi[r], preferred_element_type=jnp.float32)
                grad += jnp.dot(packed, gram_lo[r], preferred_element_type=jnp.float32)
            grad *= inverse
            grads[r] = grad
            square = grad * grad
            folded = square[:, :size]
            for k in range(1, slot_count):
                folded += square[:, k * size : (k + 1) * size]
            return total + jnp.sum(folded.reshape(size // 8, 8, size), axis=0)

        near[step, 0] = lax.fori_loop(
            0, share, descend, jnp.zeros((8, size), jnp.float32), unroll=True
        )
        copies = [
            remote(near.at[step, 0], near.at[step, d], near_send.at[step, d], near_recv.at[step, d], near_peer(d))
            for d in range(1, group)
        ]
        if step == 0:
            add_gram(CHUNKS - 1)
            lax.fori_loop(0, share, split, 0, unroll=True)
        for copy in copies:
            copy.wait_recv()
        total = near[step, 0]
        for d in range(1, group):
            total += near[step, d]
        far[step, 0] = total
        copies = [
            remote(far.at[step, 0], far.at[step, d], far_send.at[step, d], far_recv.at[step, d], far_peer(d))
            for d in range(1, layers)
        ]
        for copy in copies:
            copy.wait_recv()
        for d in range(1, layers):
            total += far[step, d]
        mean_sq = jnp.sum(jnp.sum(total, axis=0, keepdims=True), axis=1, keepdims=True) / entries
        step_size = STEP_SCALE / jnp.sqrt(mean_sq + EPSILON)

        def advance(r, carry):
            for k in range(slot_count):
                lanes = slice(k * size, (k + 1) * size)
                stepped = iterate[r, :, lanes] - step_size * grads[r, :, lanes]
                value = stepped - jnp.clip(stepped, -THRESHOLD, THRESHOLD)
                if k == 0:
                    lifted = 0.5 * (stepped + jnp.sqrt(stepped * stepped + 4.0 * step_size))
                    value = jnp.where(diagonal, lifted, value)
                if step + 1 < ITERS:
                    iterate[r, :, lanes] = value
                else:
                    out_ref[r, k] = value
            return carry

        lax.fori_loop(0, share, advance, 0, unroll=True)

    for copy in pending:
        copy.wait_send()


def body(observed, pattern, omega_init):
    var_count = lax.axis_size("var")
    samp_count = lax.axis_size("samp")
    row_blocks, slot_count, size, _ = omega_init.shape
    share = row_blocks // samp_count
    sample_rows = observed.shape[0]
    depth = sample_rows // (2 * CHUNKS)
    width = slot_count * size
    group = 4 * samp_count
    layers = var_count // 4
    dma = pltpu.SemaphoreType.DMA
    pattern = pattern.T
    scratch = [pltpu.VMEM((8 * row_blocks, depth, size), jnp.bfloat16) for _ in range(CHUNKS)]
    pick_shape = (2, samp_count, CHUNKS, slot_count - 1, share, depth, size)
    scratch += [
        pltpu.VMEM((row_blocks, sample_rows, size), jnp.bfloat16),
        pltpu.VMEM((samp_count, share, sample_rows, size), jnp.bfloat16),
        pltpu.VMEM(pick_shape, jnp.bfloat16),
        pltpu.VMEM(pick_shape, jnp.bfloat16),
        pltpu.VMEM((share, slot_count, size, size), jnp.bfloat16),
        pltpu.VMEM((2, slot_count, row_blocks), jnp.int32),
        pltpu.SMEM((2, slot_count, row_blocks), jnp.int32),
        pltpu.SMEM((2, samp_count, slot_count, share), jnp.int32),
        pltpu.VMEM((share, width, width), jnp.bfloat16),
        pltpu.VMEM((share, width, width), jnp.bfloat16),
        pltpu.VMEM((share, width, width), jnp.float32),
        pltpu.VMEM((share, size, width), jnp.float32),
        pltpu.VMEM((share, size, width), jnp.float32),
        pltpu.VMEM((ITERS, group, 8, size), jnp.float32),
        pltpu.VMEM((ITERS, layers, 8, size), jnp.float32),
        dma((row_blocks + 3,)),
        dma((1,)),
        dma((1,)),
        dma((CHUNKS,)),
        dma((CHUNKS,)),
        dma((CHUNKS, 2)),
        dma((CHUNKS, 2)),
        dma((CHUNKS,)),
        dma((CHUNKS,)),
        dma((samp_count,)),
        dma((samp_count,)),
        dma((2, samp_count, CHUNKS)),
        dma((2, samp_count, CHUNKS)),
        dma((ITERS, group)),
        dma((ITERS, group)),
        dma((ITERS, layers)),
        dma((ITERS, layers)),
    ]
    hbm = pl.BlockSpec(memory_space=pltpu.HBM)
    return pl.pallas_call(
        functools.partial(kernel, var_count, samp_count),
        out_shape=jax.ShapeDtypeStruct((share, slot_count, size, size), jnp.float32),
        in_specs=[hbm, hbm, hbm],
        out_specs=pl.BlockSpec(memory_space=pltpu.VMEM),
        scratch_shapes=scratch,
        compiler_params=pltpu.CompilerParams(
            collective_id=0, has_side_effects=True, vmem_limit_bytes=53 * 1024 * 1024
        ),
    )(observed, pattern, omega_init)


def solution(mesh):
    return jax.shard_map(
        body,
        mesh=mesh,
        in_specs=(P("samp", "var"), P("var", None), P("var", None, None, None)),
        out_specs=P(("var", "samp"), None, None, None),
        check_vma=False,
    )
```

```python
import functools

import jax
import jax.numpy as jnp
from jax import lax
from jax.experimental import pallas as pl
from jax.experimental.pallas import tpu as pltpu
from jax.sharding import PartitionSpec as P

ITERS = 2


STEP_SCALE = 0.5
THRESHOLD = 0.25
EPSILON = 1e-06
CHUNKS = 8
AHEAD = 2


def kernel(
    var_count,
    samp_count,
    obs_ref,
    pattern_ref,
    omega_ref,
    out_ref,
    *scratch,
):
    strips = scratch[:CHUNKS]
    (
        mine,
        theirs,
        staged,
        picked,
        omega,
        table,
        routes,
        slots,
        gram_hi,
        gram_lo,
        gram,
        iterate,
        grads,
        near,
        far,
        load_sem,
        table_send,
        table_recv,
        x_send,
        x_recv,
        z_send,
        z_recv,
        mate_send,
        mate_recv,
        own_send,
        own_recv,
        pick_send,
        pick_recv,
        near_send,
        near_recv,
        far_send,
        far_recv,
    ) = scratch[CHUNKS:]
    v = lax.axis_index("var")
    s = lax.axis_index("samp")
    row_blocks, slot_count, size, _ = omega_ref.shape
    share = row_blocks // samp_count
    depth = strips[0].shape[1]
    half = depth * CHUNKS
    width = slot_count * size
    inverse = 1.0 / (obs_ref.shape[0] * samp_count)
    entries = row_blocks * slot_count * size * size * var_count
    core = lax.rem(v, 2)
    x = lax.rem(v, 4) // 2
    group = 4 * samp_count
    layers = var_count // 4
    place = lax.rem(v, 4) * samp_count + s
    layer = v // 4

    def device(var, samp):
        return {"var": var, "samp": samp}

    def near_peer(d):
        other = lax.rem(place + d, group)
        return device(layer * 4 + other // samp_count, lax.rem(other, samp_count))

    def far_peer(d):
        return device(lax.rem(layer + d, layers) * 4 + lax.rem(v, 4), s)

    mate = v + 1 - 2 * core
    across = v + 2 - 4 * x

    barrier = pltpu.get_barrier_semaphore()
    for d in range(1, group):
        pl.semaphore_signal(barrier, inc=1, device_id=near_peer(d), device_id_type=pl.DeviceIdType.MESH)
    for d in range(1, layers):
        pl.semaphore_signal(barrier, inc=1, device_id=far_peer(d), device_id_type=pl.DeviceIdType.MESH)

    loads = [
        pltpu.make_async_copy(obs_ref.at[:, pl.ds(b * size, size)], mine.at[b], load_sem.at[b])
        for b in range(row_blocks)
    ]
    load_table = pltpu.make_async_copy(pattern_ref, table.at[0], load_sem.at[row_blocks])
    load_omega = pltpu.make_async_copy(
        omega_ref.at[pl.ds(s * share, share)], omega, load_sem.at[row_blocks + 1]
    )
    load_table.start()
    for copy in loads:
        copy.start()
    load_omega.start()

    pending = []

    def remote(src, dst, send, recv, target):
        copy = pltpu.make_async_remote_copy(
            src_ref=src,
            dst_ref=dst,
            send_sem=send,
            recv_sem=recv,
            device_id=target,
            device_id_type=pl.DeviceIdType.MESH,
        )
        copy.start()
        pending.append(copy)
        return copy

    def strip(c, slot):
        return strips[c].at[pl.ds(slot * row_blocks, row_blocks)]

    def samples(side, c):
        return pl.ds(pl.multiple_of(side * half + c * depth, depth), depth)

    own_slot = core * 4 + 1 + x
    across_slot = core * 4 + 2 - x

    for copy in loads:
        copy.wait()
    pl.semaphore_wait(barrier, group - 1 + layers - 1)
    load_table.wait()
    table_copy = remote(table.at[0], table.at[1], table_send.at[0], table_recv.at[0], device(across, s))
    x_copies = []
    z_copies = []
    mate_copies = []

    def begin(c):
        x_copies.append(
            remote(mine.at[:, samples(1 - x, c)], strip(c, own_slot), x_send.at[c], x_recv.at[c], device(across, s))
        )
        strips[c][pl.ds(own_slot * row_blocks, row_blocks)] = mine[:, samples(x, c)]
        target = lax.rem(layer + layers - 1 + 2 * x, layers) * 4 + lax.rem(v, 4)
        z_copies.append(
            [
                remote(
                    strip(c, own_slot), strip(c, core * 4 + 3 - 3 * x), z_send.at[c, 0], z_recv.at[c, 0], device(target, s)
                )
            ]
        )

    for c in range(AHEAD):
        begin(c)
    own_copies = []
    for d in range(1, samp_count):
        peer = lax.rem(s + d, samp_count)
        own_copies.append(
            remote(mine.at[pl.ds(peer * share, share)], theirs.at[d], own_send.at[d], own_recv.at[d], device(v, peer))
        )

    def pass_on(c):
        x_copies[c].wait_recv()
        target = lax.rem(layer + layers + 1 - 2 * x, layers) * 4 + lax.rem(v, 4)
        z_copies[c].append(
            remote(strip(c, across_slot), strip(c, core * 4 + 3 * x), z_send.at[c, 1], z_recv.at[c, 1], device(target, s))
        )
        for later in range(AHEAD * (c + 1), min(AHEAD * (c + 2), CHUNKS)):
            begin(later)

    def share_layers(c):
        for copy in z_copies[c]:
            copy.wait_recv()
        all_mine = strips[c].at[pl.ds(core * 4 * row_blocks, 4 * row_blocks)]
        mate_copies.append(remote(all_mine, all_mine, mate_send.at[c], mate_recv.at[c], device(mate, s)))

    def block_of(e, row, k):
        column = routes[e, k, row]
        offset = lax.rem(column // row_blocks - layer * 4 + var_count + 2, var_count)
        offset = jnp.minimum(offset, 7)
        return (lax.rem(offset, 2) * 4 + offset // 2) * row_blocks + lax.rem(column, row_blocks)

    picks = []

    def pick(c):
        mate_copies[c].wait_recv()
        sent = []
        for e, d in [(1 - e, samp_count - 1 - d) for e in range(2) for d in range(samp_count)]:
            peer = lax.rem(s + d, samp_count)
            for r in range(share):
                for k in range(1, slot_count):
                    block = strips[c][slots[e, d, k, r]]
                    if e == 0 and d == 0:
                        picked[0, 0, c, k - 1, r] = block
                    else:
                        staged[e, d, c, k - 1, r] = block
            if e or d:
                sent.append(
                    remote(
                        staged.at[e, d, c],
                        picked.at[e, d, c],
                        pick_send.at[e, d, c],
                        pick_recv.at[e, d, c],
                        device(across if e else v, peer),
                    )
                )
        picks.append(sent)

    def take(c, r):
        parts = []
        for e in range(2):
            rows = samples(1 - x if e else x, c)
            for d in range(samp_count):
                row_block = theirs[d, r, rows] if d else mine[s * share + r, rows]
                parts.append(
                    jnp.concatenate([row_block] + [picked[e, d, c, k, r] for k in range(slot_count - 1)], axis=1)
                )
        return jnp.concatenate(parts, axis=0)

    def add_grad(c):
        if c == 0:
            for copy in own_copies:
                copy.wait_recv()
        for copy in picks[c]:
            copy.wait_recv()
        for r in range(share):
            taken = take(c, r)
            packed = jnp.concatenate([omega[r, k] for k in range(slot_count)], axis=1)
            weighted = lax.dot_general(
                packed, taken, (((1,), (1,)), ((), ())), preferred_element_type=jnp.float32
            ).astype(jnp.bfloat16)
            grad = jnp.dot(weighted, taken, preferred_element_type=jnp.float32)
            if c == 0:
                grads[r] = grad
            else:
                grads[r] += grad

    def add_gram(c):
        for r in range(share):
            taken = take(c, r)
            product = lax.dot_general(
                taken, taken, (((0,), (0,)), ((), ())), preferred_element_type=jnp.float32
            )
            if c == 0:
                gram[r] = product
            else:
                gram[r] += product

    table_copy.wait_recv()
    fetch = pltpu.make_async_copy(table, routes, load_sem.at[row_blocks + 2])
    fetch.start()
    fetch.wait()
    for e in range(2):
        for d in range(samp_count):
            for k in range(1, slot_count):
                for r in range(share):
                    slots[e, d, k, r] = block_of(e, lax.rem(s + d, samp_count) * share + r, k)
    load_omega.wait()

    for turn in range(CHUNKS + 5):
        if turn < CHUNKS:
            pass_on(turn)
        if 0 <= turn - 2 < CHUNKS:
            share_layers(turn - 2)
        if 0 <= turn - 3 < CHUNKS:
            pick(turn - 3)
        if 0 <= turn - 5 < CHUNKS:
            add_grad(turn - 5)
            if turn - 5 < CHUNKS - 1:
                add_gram(turn - 5)

    def split(r, carry):
        full = gram[r]
        high = full.astype(jnp.bfloat16)
        gram_hi[r] = high
        gram_lo[r] = (full - high.astype(jnp.float32)).astype(jnp.bfloat16)
        for k in range(slot_count):
            iterate[r, :, k * size : (k + 1) * size] = omega[r, k].astype(jnp.float32)
        return carry

    rows = lax.broadcasted_iota(jnp.int32, (size, size), 0)
    columns = lax.broadcasted_iota(jnp.int32, (size, size), 1)
    diagonal = rows == columns

    for step in range(ITERS):

        def descend(r, total):
            if step == 0:
                grad = grads[r]
            else:
                packed = iterate[r].astype(jnp.bfloat16)
                grad = jnp.dot(packed, gram_hi[r], preferred_element_type=jnp.float32)
                grad += jnp.dot(packed, gram_lo[r], preferred_element_type=jnp.float32)
            grad *= inverse
            grads[r] = grad
            square = grad * grad
            folded = square[:, :size]
            for k in range(1, slot_count):
                folded += square[:, k * size : (k + 1) * size]
            return total + jnp.sum(folded.reshape(size // 8, 8, size), axis=0)

        near[step, 0] = lax.fori_loop(
            0, share, descend, jnp.zeros((8, size), jnp.float32), unroll=True
        )
        copies = [
            remote(near.at[step, 0], near.at[step, d], near_send.at[step, d], near_recv.at[step, d], near_peer(d))
            for d in range(1, group)
        ]
        if step == 0:
            add_gram(CHUNKS - 1)
            lax.fori_loop(0, share, split, 0, unroll=True)
        for copy in copies:
            copy.wait_recv()
        total = near[step, 0]
        for d in range(1, group):
            total += near[step, d]
        far[step, 0] = total
        copies = [
            remote(far.at[step, 0], far.at[step, d], far_send.at[step, d], far_recv.at[step, d], far_peer(d))
            for d in range(1, layers)
        ]
        for copy in copies:
            copy.wait_recv()
        for d in range(1, layers):
            total += far[step, d]
        mean_sq = jnp.sum(jnp.sum(total, axis=0, keepdims=True), axis=1, keepdims=True) / entries
        step_size = STEP_SCALE / jnp.sqrt(mean_sq + EPSILON)

        def advance(r, carry):
            for k in range(slot_count):
                lanes = slice(k * size, (k + 1) * size)
                stepped = iterate[r, :, lanes] - step_size * grads[r, :, lanes]
                value = stepped - jnp.clip(stepped, -THRESHOLD, THRESHOLD)
                if k == 0:
                    lifted = 0.5 * (stepped + jnp.sqrt(stepped * stepped + 4.0 * step_size))
                    value = jnp.where(diagonal, lifted, value)
                if step + 1 < ITERS:
                    iterate[r, :, lanes] = value
                else:
                    out_ref[r, k] = value
            return carry

        lax.fori_loop(0, share, advance, 0, unroll=True)

    for copy in pending:
        copy.wait_send()


def body(observed, pattern, omega_init):
    var_count = lax.axis_size("var")
    samp_count = lax.axis_size("samp")
    row_blocks, slot_count, size, _ = omega_init.shape
    share = row_blocks // samp_count
    sample_rows = observed.shape[0]
    depth = sample_rows // (2 * CHUNKS)
    width = slot_count * size
    group = 4 * samp_count
    layers = var_count // 4
    dma = pltpu.SemaphoreType.DMA
    pattern = pattern.T
    scratch = [pltpu.VMEM((8 * row_blocks, depth, size), jnp.bfloat16) for _ in range(CHUNKS)]
    pick_shape = (2, samp_count, CHUNKS, slot_count - 1, share, depth, size)
    scratch += [
        pltpu.VMEM((row_blocks, sample_rows, size), jnp.bfloat16),
        pltpu.VMEM((samp_count, share, sample_rows, size), jnp.bfloat16),
        pltpu.VMEM(pick_shape, jnp.bfloat16),
        pltpu.VMEM(pick_shape, jnp.bfloat16),
        pltpu.VMEM((share, slot_count, size, size), jnp.bfloat16),
        pltpu.VMEM((2, slot_count, row_blocks), jnp.int32),
        pltpu.SMEM((2, slot_count, row_blocks), jnp.int32),
        pltpu.SMEM((2, samp_count, slot_count, share), jnp.int32),
        pltpu.VMEM((share, width, width), jnp.bfloat16),
        pltpu.VMEM((share, width, width), jnp.bfloat16),
        pltpu.VMEM((share, width, width), jnp.float32),
        pltpu.VMEM((share, size, width), jnp.float32),
        pltpu.VMEM((share, size, width), jnp.float32),
        pltpu.VMEM((ITERS, group, 8, size), jnp.float32),
        pltpu.VMEM((ITERS, layers, 8, size), jnp.float32),
        dma((row_blocks + 3,)),
        dma((1,)),
        dma((1,)),
        dma((CHUNKS,)),
        dma((CHUNKS,)),
        dma((CHUNKS, 2)),
        dma((CHUNKS, 2)),
        dma((CHUNKS,)),
        dma((CHUNKS,)),
        dma((samp_count,)),
        dma((samp_count,)),
        dma((2, samp_count, CHUNKS)),
        dma((2, samp_count, CHUNKS)),
        dma((ITERS, group)),
        dma((ITERS, group)),
        dma((ITERS, layers)),
        dma((ITERS, layers)),
    ]
    hbm = pl.BlockSpec(memory_space=pltpu.HBM)
    return pl.pallas_call(
        functools.partial(kernel, var_count, samp_count),
        out_shape=jax.ShapeDtypeStruct((share, slot_count, size, size), jnp.float32),
        in_specs=[hbm, hbm, hbm],
        out_specs=pl.BlockSpec(memory_space=pltpu.VMEM),
        scratch_shapes=scratch,
        compiler_params=pltpu.CompilerParams(
            collective_id=0, has_side_effects=True, vmem_limit_bytes=53 * 1024 * 1024
        ),
    )(observed, pattern, omega_init)


def solution(mesh):
    return jax.shard_map(
        body,
        mesh=mesh,
        in_specs=(P("samp", "var"), P("var", None), P("var", None, None, None)),
        out_specs=P(("var", "samp"), None, None, None),
        check_vma=False,
    )
```

```python
import functools

import jax
import jax.numpy as jnp
from jax import lax
from jax.experimental import pallas as pl
from jax.experimental.pallas import tpu as pltpu
from jax.sharding import PartitionSpec as P

ITERS = 2


STEP_SCALE = 0.5
THRESHOLD = 0.25
EPSILON = 1e-06
CHUNKS = 8
AHEAD = 8


def kernel(
    var_count,
    samp_count,
    obs_ref,
    pattern_ref,
    omega_ref,
    out_ref,
    *scratch,
):
    strips = scratch[:CHUNKS]
    (
        mine,
        theirs,
        staged,
        picked,
        omega,
        table,
        routes,
        slots,
        gram_hi,
        gram_lo,
        gram,
        iterate,
        grads,
        near,
        far,
        load_sem,
        table_send,
        table_recv,
        x_send,
        x_recv,
        z_send,
        z_recv,
        mate_send,
        mate_recv,
        own_send,
        own_recv,
        pick_send,
        pick_recv,
        near_send,
        near_recv,
        far_send,
        far_recv,
    ) = scratch[CHUNKS:]
    v = lax.axis_index("var")
    s = lax.axis_index("samp")
    row_blocks, slot_count, size, _ = omega_ref.shape
    share = row_blocks // samp_count
    depth = strips[0].shape[1]
    half = depth * CHUNKS
    width = slot_count * size
    inverse = 1.0 / (obs_ref.shape[0] * samp_count)
    entries = row_blocks * slot_count * size * size * var_count
    core = lax.rem(v, 2)
    x = lax.rem(v, 4) // 2
    group = 4 * samp_count
    layers = var_count // 4
    place = lax.rem(v, 4) * samp_count + s
    layer = v // 4

    def device(var, samp):
        return {"var": var, "samp": samp}

    def near_peer(d):
        other = lax.rem(place + d, group)
        return device(layer * 4 + other // samp_count, lax.rem(other, samp_count))

    def far_peer(d):
        return device(lax.rem(layer + d, layers) * 4 + lax.rem(v, 4), s)

    mate = v + 1 - 2 * core
    across = v + 2 - 4 * x

    barrier = pltpu.get_barrier_semaphore()
    for d in range(1, group):
        pl.semaphore_signal(barrier, inc=1, device_id=near_peer(d), device_id_type=pl.DeviceIdType.MESH)
    for d in range(1, layers):
        pl.semaphore_signal(barrier, inc=1, device_id=far_peer(d), device_id_type=pl.DeviceIdType.MESH)

    loads = [
        pltpu.make_async_copy(obs_ref.at[:, pl.ds(b * size, size)], mine.at[b], load_sem.at[b])
        for b in range(row_blocks)
    ]
    load_table = pltpu.make_async_copy(pattern_ref, table.at[0], load_sem.at[row_blocks])
    load_omega = pltpu.make_async_copy(
        omega_ref.at[pl.ds(s * share, share)], omega, load_sem.at[row_blocks + 1]
    )
    load_table.start()
    for copy in loads:
        copy.start()
    load_omega.start()

    pending = []

    def remote(src, dst, send, recv, target):
        copy = pltpu.make_async_remote_copy(
            src_ref=src,
            dst_ref=dst,
            send_sem=send,
            recv_sem=recv,
            device_id=target,
            device_id_type=pl.DeviceIdType.MESH,
        )
        copy.start()
        pending.append(copy)
        return copy

    def strip(c, slot):
        return strips[c].at[pl.ds(slot * row_blocks, row_blocks)]

    def samples(side, c):
        return pl.ds(pl.multiple_of(side * half + c * depth, depth), depth)

    own_slot = core * 4 + 1 + x
    across_slot = core * 4 + 2 - x

    for copy in loads:
        copy.wait()
    pl.semaphore_wait(barrier, group - 1 + layers - 1)
    load_table.wait()
    table_copy = remote(table.at[0], table.at[1], table_send.at[0], table_recv.at[0], device(across, s))
    x_copies = []
    z_copies = []
    mate_copies = []

    def begin(c):
        x_copies.append(
            remote(mine.at[:, samples(1 - x, c)], strip(c, own_slot), x_send.at[c], x_recv.at[c], device(across, s))
        )
        strips[c][pl.ds(own_slot * row_blocks, row_blocks)] = mine[:, samples(x, c)]
        target = lax.rem(layer + layers - 1 + 2 * x, layers) * 4 + lax.rem(v, 4)
        z_copies.append(
            [
                remote(
                    strip(c, own_slot), strip(c, core * 4 + 3 - 3 * x), z_send.at[c, 0], z_recv.at[c, 0], device(target, s)
                )
            ]
        )

    for c in range(AHEAD):
        begin(c)
    own_copies = []
    for d in range(1, samp_count):
        peer = lax.rem(s + d, samp_count)
        own_copies.append(
            remote(mine.at[pl.ds(peer * share, share)], theirs.at[d], own_send.at[d], own_recv.at[d], device(v, peer))
        )

    def pass_on(c):
        x_copies[c].wait_recv()
        target = lax.rem(layer + layers + 1 - 2 * x, layers) * 4 + lax.rem(v, 4)
        z_copies[c].append(
            remote(strip(c, across_slot), strip(c, core * 4 + 3 * x), z_send.at[c, 1], z_recv.at[c, 1], device(target, s))
        )
        for later in range(AHEAD * (c + 1), min(AHEAD * (c + 2), CHUNKS)):
            begin(later)

    def share_layers(c):
        for copy in z_copies[c]:
            copy.wait_recv()
        all_mine = strips[c].at[pl.ds(core * 4 * row_blocks, 4 * row_blocks)]
        mate_copies.append(remote(all_mine, all_mine, mate_send.at[c], mate_recv.at[c], device(mate, s)))

    def block_of(e, row, k):
        column = routes[e, k, row]
        offset = lax.rem(column // row_blocks - layer * 4 + var_count + 2, var_count)
        offset = jnp.minimum(offset, 7)
        return (lax.rem(offset, 2) * 4 + offset // 2) * row_blocks + lax.rem(column, row_blocks)

    picks = []

    def pick(c):
        mate_copies[c].wait_recv()
        sent = []
        for e, d in [(1 - e, samp_count - 1 - d) for e in range(2) for d in range(samp_count)]:
            peer = lax.rem(s + d, samp_count)
            for r in range(share):
                for k in range(1, slot_count):
                    block = strips[c][slots[e, d, k, r]]
                    if e == 0 and d == 0:
                        picked[0, 0, c, k - 1, r] = block
                    else:
                        staged[e, d, c, k - 1, r] = block
            if e or d:
                sent.append(
                    remote(
                        staged.at[e, d, c],
                        picked.at[e, d, c],
                        pick_send.at[e, d, c],
                        pick_recv.at[e, d, c],
                        device(across if e else v, peer),
                    )
                )
        picks.append(sent)

    def take(c, r):
        parts = []
        for e in range(2):
            rows = samples(1 - x if e else x, c)
            for d in range(samp_count):
                row_block = theirs[d, r, rows] if d else mine[s * share + r, rows]
                parts.append(
                    jnp.concatenate([row_block] + [picked[e, d, c, k, r] for k in range(slot_count - 1)], axis=1)
                )
        return jnp.concatenate(parts, axis=0)

    def add_grad(c):
        if c == 0:
            for copy in own_copies:
                copy.wait_recv()
        for copy in picks[c]:
            copy.wait_recv()
        for r in range(share):
            taken = take(c, r)
            packed = jnp.concatenate([omega[r, k] for k in range(slot_count)], axis=1)
            weighted = lax.dot_general(
                packed, taken, (((1,), (1,)), ((), ())), preferred_element_type=jnp.float32
            ).astype(jnp.bfloat16)
            grad = jnp.dot(weighted, taken, preferred_element_type=jnp.float32)
            if c == 0:
                grads[r] = grad
            else:
                grads[r] += grad

    def add_gram(c):
        for r in range(share):
            taken = take(c, r)
            product = lax.dot_general(
                taken, taken, (((0,), (0,)), ((), ())), preferred_element_type=jnp.float32
            )
            if c == 0:
                gram[r] = product
            else:
                gram[r] += product

    table_copy.wait_recv()
    fetch = pltpu.make_async_copy(table, routes, load_sem.at[row_blocks + 2])
    fetch.start()
    fetch.wait()
    for e in range(2):
        for d in range(samp_count):
            for k in range(1, slot_count):
                for r in range(share):
                    slots[e, d, k, r] = block_of(e, lax.rem(s + d, samp_count) * share + r, k)
    load_omega.wait()

    for turn in range(CHUNKS + 5):
        if turn < CHUNKS:
            pass_on(turn)
        if 0 <= turn - 2 < CHUNKS:
            share_layers(turn - 2)
        if 0 <= turn - 3 < CHUNKS:
            pick(turn - 3)
        if 0 <= turn - 5 < CHUNKS:
            add_grad(turn - 5)
            if turn - 5 < CHUNKS - 1:
                add_gram(turn - 5)

    def split(r, carry):
        full = gram[r]
        high = full.astype(jnp.bfloat16)
        gram_hi[r] = high
        gram_lo[r] = (full - high.astype(jnp.float32)).astype(jnp.bfloat16)
        for k in range(slot_count):
            iterate[r, :, k * size : (k + 1) * size] = omega[r, k].astype(jnp.float32)
        return carry

    rows = lax.broadcasted_iota(jnp.int32, (size, size), 0)
    columns = lax.broadcasted_iota(jnp.int32, (size, size), 1)
    diagonal = rows == columns

    for step in range(ITERS):

        def descend(r, total):
            if step == 0:
                grad = grads[r]
            else:
                packed = iterate[r].astype(jnp.bfloat16)
                grad = jnp.dot(packed, gram_hi[r], preferred_element_type=jnp.float32)
                grad += jnp.dot(packed, gram_lo[r], preferred_element_type=jnp.float32)
            grad *= inverse
            grads[r] = grad
            square = grad * grad
            folded = square[:, :size]
            for k in range(1, slot_count):
                folded += square[:, k * size : (k + 1) * size]
            return total + jnp.sum(folded.reshape(size // 8, 8, size), axis=0)

        near[step, 0] = lax.fori_loop(
            0, share, descend, jnp.zeros((8, size), jnp.float32), unroll=True
        )
        copies = [
            remote(near.at[step, 0], near.at[step, d], near_send.at[step, d], near_recv.at[step, d], near_peer(d))
            for d in range(1, group)
        ]
        if step == 0:
            add_gram(CHUNKS - 1)
            lax.fori_loop(0, share, split, 0, unroll=True)
        for copy in copies:
            copy.wait_recv()
        total = near[step, 0]
        for d in range(1, group):
            total += near[step, d]
        far[step, 0] = total
        copies = [
            remote(far.at[step, 0], far.at[step, d], far_send.at[step, d], far_recv.at[step, d], far_peer(d))
            for d in range(1, layers)
        ]
        for copy in copies:
            copy.wait_recv()
        for d in range(1, layers):
            total += far[step, d]
        mean_sq = jnp.sum(jnp.sum(total, axis=0, keepdims=True), axis=1, keepdims=True) / entries
        step_size = STEP_SCALE / jnp.sqrt(mean_sq + EPSILON)

        def advance(r, carry):
            for k in range(slot_count):
                lanes = slice(k * size, (k + 1) * size)
                stepped = iterate[r, :, lanes] - step_size * grads[r, :, lanes]
                value = stepped - jnp.clip(stepped, -THRESHOLD, THRESHOLD)
                if k == 0:
                    lifted = 0.5 * (stepped + jnp.sqrt(stepped * stepped + 4.0 * step_size))
                    value = jnp.where(diagonal, lifted, value)
                if step + 1 < ITERS:
                    iterate[r, :, lanes] = value
                else:
                    out_ref[r, k] = value
            return carry

        lax.fori_loop(0, share, advance, 0, unroll=True)

    for copy in pending:
        copy.wait_send()


def body(observed, pattern, omega_init):
    var_count = lax.axis_size("var")
    samp_count = lax.axis_size("samp")
    row_blocks, slot_count, size, _ = omega_init.shape
    share = row_blocks // samp_count
    sample_rows = observed.shape[0]
    depth = sample_rows // (2 * CHUNKS)
    width = slot_count * size
    group = 4 * samp_count
    layers = var_count // 4
    dma = pltpu.SemaphoreType.DMA
    pattern = pattern.T
    scratch = [pltpu.VMEM((8 * row_blocks, depth, size), jnp.bfloat16) for _ in range(CHUNKS)]
    pick_shape = (2, samp_count, CHUNKS, slot_count - 1, share, depth, size)
    scratch += [
        pltpu.VMEM((row_blocks, sample_rows, size), jnp.bfloat16),
        pltpu.VMEM((samp_count, share, sample_rows, size), jnp.bfloat16),
        pltpu.VMEM(pick_shape, jnp.bfloat16),
        pltpu.VMEM(pick_shape, jnp.bfloat16),
        pltpu.VMEM((share, slot_count, size, size), jnp.bfloat16),
        pltpu.VMEM((2, slot_count, row_blocks), jnp.int32),
        pltpu.SMEM((2, slot_count, row_blocks), jnp.int32),
        pltpu.SMEM((2, samp_count, slot_count, share), jnp.int32),
        pltpu.VMEM((share, width, width), jnp.bfloat16),
        pltpu.VMEM((share, width, width), jnp.bfloat16),
        pltpu.VMEM((share, width, width), jnp.float32),
        pltpu.VMEM((share, size, width), jnp.float32),
        pltpu.VMEM((share, size, width), jnp.float32),
        pltpu.VMEM((ITERS, group, 8, size), jnp.float32),
        pltpu.VMEM((ITERS, layers, 8, size), jnp.float32),
        dma((row_blocks + 3,)),
        dma((1,)),
        dma((1,)),
        dma((CHUNKS,)),
        dma((CHUNKS,)),
        dma((CHUNKS, 2)),
        dma((CHUNKS, 2)),
        dma((CHUNKS,)),
        dma((CHUNKS,)),
        dma((samp_count,)),
        dma((samp_count,)),
        dma((2, samp_count, CHUNKS)),
        dma((2, samp_count, CHUNKS)),
        dma((ITERS, group)),
        dma((ITERS, group)),
        dma((ITERS, layers)),
        dma((ITERS, layers)),
    ]
    hbm = pl.BlockSpec(memory_space=pltpu.HBM)
    return pl.pallas_call(
        functools.partial(kernel, var_count, samp_count),
        out_shape=jax.ShapeDtypeStruct((share, slot_count, size, size), jnp.float32),
        in_specs=[hbm, hbm, hbm],
        out_specs=pl.BlockSpec(memory_space=pltpu.VMEM),
        scratch_shapes=scratch,
        compiler_params=pltpu.CompilerParams(
            collective_id=0, has_side_effects=True, vmem_limit_bytes=53 * 1024 * 1024
        ),
    )(observed, pattern, omega_init)


def solution(mesh):
    return jax.shard_map(
        body,
        mesh=mesh,
        in_specs=(P("samp", "var"), P("var", None), P("var", None, None, None)),
        out_specs=P(("var", "samp"), None, None, None),
        check_vma=False,
    )
```
